512 devices in a mesh: level: 16 (over z_hi, y), req: 32 (over z_lo, x, core).
Axes of the slice: x: 4, y: 8, z: 8 (z_hi: 2, z_lo: 4; z = z_hi * 4 + z_lo), core: 2. Of those that a mesh axis runs over, the one named last changes fastest.
Arguments:
- queries: bfloat16 [256, 256, 896], P('level', 'req'), may hold values from -120 to 120
- out_grad: bfloat16 [256, 256, 896], P('level', 'req'), may hold values from -5 to 5
- resp_key: bfloat16 [256, 256, 128], P('level', 'req'), may hold values from -4 to 4
- resp_value: bfloat16 [256, 256, 128], P('level', 'req'), may hold values from -4 to 4
- sys_key: bfloat16 [512, 128], P('level'), may hold values from -4 to 4
- sys_value: bfloat16 [512, 128], P('level'), may hold values from -4 to 4
- ctx_key: bfloat16 [64, 512, 128], P('req', 'level'), may hold values from -4 to 4
- ctx_value: bfloat16 [64, 512, 128], P('req', 'level'), may hold values from -4 to 4
- parent: int32 [256], P('req'), may hold values from 0 to 63, as said below
- resp_len: int32 [256], P('req'), may hold values from 64 to 256
- ctx_len: int32 [64], P('req'), may hold values from 128 to 512
Outputs:
- d_queries: float32 [256, 256, 896], P('level', 'req')
- d_sys_key: float32 [512, 128], P(('level', 'req'))
- d_sys_value: float32 [512, 128], P(('level', 'req'))
- d_ctx_key: float32 [64, 512, 128], P('req', 'level')
- d_ctx_value: float32 [64, 512, 128], P('req', 'level')
- d_resp_key: float32 [256, 256, 128], P('level', 'req')
- d_resp_value: float32 [256, 256, 128], P('level', 'req')
The draws below stay inside these ranges and needn't reach their ends.
Inputs may be any that keep to these rules, and one draw needn't show every extreme that they name: Response i's parent is one of the contexts (i // 8) * 2 to (i // 8 + 1) * 2 - 1.
All inputs are finite; a program needn't handle non-finite values.
Results may differ from the reference program's by a relative error of at most 0.0049.
Values may be sent and summed in bfloat16 or wider, within the bound.
No kernel may reach another device: no remote copies, remote signals or barrier semaphores. Data moves between devices by JAX's collectives and lax.ppermute only.
A program may use at most 64 MiB of HBM per device.

```python
import jax
import jax.numpy as jnp
from jax import lax

HEADS = 7
HEAD_DIM = 128
CH = 256
CTX_PER = 2
RESP_DEV = 8
RESP = 256
SYS = 512
CTX = 512
CTXS = 64


def base_keys(key):
    return jax.random.truncated_normal(jax.random.fold_in(key, 500), -4.0, 4.0, (SYS, HEAD_DIM), jnp.float32)


def draw_sys_key(key, part):
    shared = base_keys(key)
    return shared.astype(jnp.bfloat16)


def draw_queries(key, part):
    key = jax.random.fold_in(key, 2)
    return jax.random.truncated_normal(key, -4.0, 4.0, (CH, RESP, HEADS * HEAD_DIM), jnp.float32).astype(jnp.bfloat16)


def draw_parent(key, part):
    key = jax.random.fold_in(key, 3)
    owners = jnp.arange(RESP, dtype=jnp.int32) // RESP_DEV
    picks = jax.random.randint(key, (RESP,), 0, CTX_PER, jnp.int32)
    chosen = owners * CTX_PER + picks
    chosen = chosen.at[0].set(0)
    chosen = chosen.at[RESP - 1].set(CTXS - 1)
    return chosen


def draw_resp_len(key, part):
    key = jax.random.fold_in(key, 4)
    lengths = jax.random.randint(key, (RESP,), CH // 4, CH + 1, jnp.int32)
    lengths = lengths.at[0].set(CH)
    lengths = lengths.at[1].set(CH // 4)
    return lengths


def draw_ctx_len(key, part):
    key = jax.random.fold_in(key, 5)
    lengths = jax.random.randint(key, (CTXS,), CTX // 4, CTX + 1, jnp.int32)
    lengths = lengths.at[0].set(CTX)
    lengths = lengths.at[1].set(CTX // 4)
    return lengths


def levels(own_key, shape, pieces, least, top_value):
    gain = 1.0
    for axis_at, shards_of in pieces:
        steps = jax.random.uniform(jax.random.fold_in(jax.random.fold_in(own_key, 6), axis_at), (shards_of,), jnp.float32, least / len(pieces), top_value / len(pieces))
        gain = gain * jnp.repeat(jnp.exp(steps), shape[axis_at] // shards_of).reshape((-1,) + (1,) * (len(shape) - 1 - axis_at))
    return gain


def gaussian(stream_key, extent, width, bound, pieces=(), kind=jnp.bfloat16):
    drawn = width * jax.random.normal(stream_key, extent, jnp.float32)
    if pieces:
        drawn = drawn * levels(stream_key, extent, pieces, -0.22, 0.18)
    return jnp.clip(drawn, -bound, bound).astype(kind)


def setup_inputs(seed: int = 0) -> dict:
    key_of = jax.random.split(jax.random.key(seed), 12)
    queries = draw_queries(jax.random.fold_in(key_of[11], 71), 0)
    out_grad = gaussian(key_of[1], (CH, RESP, HEADS * HEAD_DIM), 1.0, 5.0, ((0, 16), (1, 32)))
    resp_key = gaussian(key_of[2], (CH, RESP, HEAD_DIM), 1.0, 4.0, ((0, 16), (1, 32)))
    resp_value = gaussian(key_of[3], (CH, RESP, HEAD_DIM), 1.0, 4.0, ((0, 16), (1, 32)))
    sys_key = draw_sys_key(jax.random.fold_in(key_of[11], 71), 0)
    sys_value = gaussian(key_of[5], (SYS, HEAD_DIM), 1.0, 4.0, ((0, 16),))
    ctx_key = gaussian(key_of[6], (CTXS, CTX, HEAD_DIM), 1.0, 4.0, ((0, 32), (1, 16)))
    ctx_value = gaussian(key_of[7], (CTXS, CTX, HEAD_DIM), 1.0, 4.0, ((0, 32), (1, 16)))
    parent = draw_parent(jax.random.fold_in(key_of[11], 71), 0)
    resp_len = draw_resp_len(jax.random.fold_in(key_of[11], 71), 0)
    ctx_len = draw_ctx_len(jax.random.fold_in(key_of[11], 71), 0)
    return dict(queries=queries, out_grad=out_grad, resp_key=resp_key, resp_value=resp_value, sys_key=sys_key, sys_value=sys_value, ctx_key=ctx_key, ctx_value=ctx_value, parent=parent, resp_len=resp_len, ctx_len=ctx_len)


NEGATIVE = -1.0e30


def one_response(queries_one, grads_one, key_rows, value_rows, allowed):
    scaling = HEAD_DIM ** -0.5
    key_float = key_rows.astype(jnp.float32)
    value_float = value_rows.astype(jnp.float32)
    query_float = queries_one.astype(jnp.float32)
    grad_float = grads_one.astype(jnp.float32)
    scores = jnp.einsum("kd,thd->kht", key_float, query_float) * scaling
    maxima = jnp.max(jnp.where(allowed, scores, NEGATIVE), axis=0)
    totals = jnp.sum(jnp.where(allowed, jnp.exp(scores - maxima[None]), 0.0), axis=0)
    logsum = maxima + jnp.log(totals)
    chances = jnp.where(allowed, jnp.exp(scores - logsum[None]), 0.0)
    attn_out = jnp.einsum("kht,kd->thd", chances, value_float, precision=lax.Precision.HIGHEST)
    deltas = jnp.sum(grad_float * attn_out, axis=2)
    products = jnp.einsum("kd,thd->kht", value_float, grad_float)
    slopes = lax.optimization_barrier((chances * (products - deltas.T[None])).astype(jnp.bfloat16))
    chances_low = lax.optimization_barrier(chances.astype(jnp.bfloat16))
    slope_float = slopes.astype(jnp.float32)
    query_grad = scaling * jnp.einsum("kht,kd->thd", slope_float, key_float)
    key_grad = scaling * jnp.einsum("kht,thd->kd", slope_float, query_float)
    value_grad = jnp.einsum("kht,thd->kd", chances_low.astype(jnp.float32), grad_float)
    return query_grad, key_grad, value_grad


def reference(queries, out_grad, resp_key, resp_value, sys_key, sys_value, ctx_key, ctx_value, parent, resp_len, ctx_len):
    rows_all = jnp.arange(CH, dtype=jnp.int32)
    ctx_places = jnp.arange(CTX, dtype=jnp.int32)
    queries_four = queries.reshape(CH, RESP, HEADS, HEAD_DIM)
    grads_four = out_grad.reshape(CH, RESP, HEADS, HEAD_DIM)
    causal = rows_all[:, None] <= rows_all[None, :]
    open_sys = jnp.ones((SYS, CH), dtype=bool)

    def visit(carried, response):
        sys_kgrad, sys_vgrad, ctx_kgrad, ctx_vgrad = carried
        owner = parent[response]
        queries_one = queries_four[:, response]
        grads_one = grads_four[:, response]
        live_rows = rows_all < resp_len[response]
        grads_one = jnp.where(live_rows[:, None, None], grads_one, jnp.zeros((), jnp.bfloat16))
        own_keys = resp_key[:, response]
        own_values = resp_value[:, response]
        key_rows = jnp.concatenate([sys_key, ctx_key[owner], own_keys], axis=0)
        value_rows = jnp.concatenate([sys_value, ctx_value[owner], own_values], axis=0)
        ctx_allowed = jnp.broadcast_to((ctx_places < ctx_len[owner])[:, None], (CTX, CH))
        allowed = jnp.concatenate([open_sys, ctx_allowed, causal], axis=0)[:, None, :]
        query_grad, key_grad, value_grad = one_response(queries_one, grads_one, key_rows, value_rows, allowed)
        sys_kgrad = sys_kgrad + key_grad[:SYS]
        sys_vgrad = sys_vgrad + value_grad[:SYS]
        ctx_kgrad = ctx_kgrad.at[owner].add(key_grad[SYS:SYS + CTX])
        ctx_vgrad = ctx_vgrad.at[owner].add(value_grad[SYS:SYS + CTX])
        return (sys_kgrad, sys_vgrad, ctx_kgrad, ctx_vgrad), (query_grad, key_grad[SYS + CTX:], value_grad[SYS + CTX:])

    initial = (jnp.zeros((SYS, HEAD_DIM), jnp.float32), jnp.zeros((SYS, HEAD_DIM), jnp.float32),
               jnp.zeros((CTXS, CTX, HEAD_DIM), jnp.float32), jnp.zeros((CTXS, CTX, HEAD_DIM), jnp.float32))
    finals, gathered = lax.scan(visit, initial, jnp.arange(RESP, dtype=jnp.int32))
    sys_kgrad, sys_vgrad, ctx_kgrad, ctx_vgrad = finals
    query_grads, own_kgrads, own_vgrads = gathered
    d_queries = jnp.transpose(query_grads, (1, 0, 2, 3)).reshape(CH, RESP, HEADS * HEAD_DIM)
    d_resp_key = jnp.transpose(own_kgrads, (1, 0, 2))
    d_resp_value = jnp.transpose(own_vgrads, (1, 0, 2))
    return (d_queries, sys_kgrad, sys_vgrad, ctx_kgrad, ctx_vgrad, d_resp_key, d_resp_value)
```

```python
import math

import jax
import jax.numpy as jnp
from jax import lax
from jax.experimental import pallas as pl
from jax.experimental.pallas import tpu as pltpu
from jax.sharding import PartitionSpec as P

HEADS = 7
HEAD_DIM = 128
CTX_PER = 2
LEVELS = 16
RESP_DEV = 8
SPAN = 16
SPLIT = LEVELS // RESP_DEV
PART = SPAN // SPLIT
SYS_ROWS = 32
CTX_ROWS = 32
SYS = SYS_ROWS * LEVELS
CTX = CTX_ROWS * LEVELS
CH = SPAN * LEVELS
KEYS = SYS + CTX + CH
QROWS = PART * HEADS
ROWS = QROWS * LEVELS
WIDTH = HEADS * HEAD_DIM
SCALING = HEAD_DIM**-0.5
NEGATIVE = -1e30
BLOCK = 128
MIB = 1 << 20

IN_Q = 0
IN_G = IN_Q + QROWS
IN_OK = IN_G + QROWS
IN_OV = IN_OK + SPAN
IN_SK = IN_OV + SPAN
IN_SV = IN_SK + SYS_ROWS
IN_CK = IN_SV + SYS_ROWS
IN_CV = IN_CK + CTX_ROWS
IN_ROWS = IN_CV + CTX_ROWS

OUT_SK = 0
OUT_SV = OUT_SK + SYS_ROWS
OUT_CK = OUT_SV + SYS_ROWS
OUT_CV = OUT_CK + CTX_ROWS
OUT_OK = OUT_CV + CTX_ROWS
OUT_OV = OUT_OK + SPAN
OUT_Q = OUT_OV + SPAN
OUT_ROWS = OUT_Q + QROWS

f32 = jnp.float32
bf16 = jnp.bfloat16


def dot(a, b, contract_a, contract_b):
    return lax.dot_general(
        a, b, (((contract_a,), (contract_b,)), ((), ())), preferred_element_type=f32
    )


def swap_matrix(rows_inner, columns_inner):
    size = rows_inner * columns_inner
    row = lax.broadcasted_iota(jnp.int32, (size, size), 0)
    column = lax.broadcasted_iota(jnp.int32, (size, size), 1)
    wanted = (row % columns_inner) * rows_inner + row // columns_inner
    return (column == wanted).astype(bf16)


def flat(ref):
    whole = ref[...].astype(f32)
    return whole.reshape(SPAN * RESP_DEV, whole.shape[2]).astype(bf16)


def pack_kernel(
    parent_ref, q_ref, g_ref, rk_ref, rv_ref, sk_ref, sv_ref, ck_ref, cv_ref, send_ref
):
    swap = swap_matrix(RESP_DEV, SPAN)
    queries = dot(swap, flat(q_ref), 1, 0)
    grads = dot(swap, flat(g_ref), 1, 0)
    own_k = dot(swap, flat(rk_ref), 1, 0).astype(bf16)
    own_v = dot(swap, flat(rv_ref), 1, 0).astype(bf16)
    sys_k = sk_ref[...]
    sys_v = sv_ref[...]
    for response in range(RESP_DEV):
        owner = lax.rem(parent_ref[response], CTX_PER)
        ctx_k = ck_ref[owner]
        ctx_v = cv_ref[owner]
        for part in range(SPLIT):
            to = response * SPLIT + part
            first = response * SPAN + part * PART
            pieces = [
                rows[first : first + PART, head * HEAD_DIM : (head + 1) * HEAD_DIM]
                for rows in (queries, grads)
                for head in range(HEADS)
            ]
            send_ref[to, IN_Q:IN_OK, :] = jnp.concatenate(pieces, axis=0).astype(bf16)
            span = slice(response * SPAN, (response + 1) * SPAN)
            send_ref[to, IN_OK:IN_OV, :] = own_k[span]
            send_ref[to, IN_OV:IN_SK, :] = own_v[span]
            send_ref[to, IN_SK:IN_SV, :] = sys_k
            send_ref[to, IN_SV:IN_CK, :] = sys_v
            send_ref[to, IN_CK:IN_CV, :] = ctx_k
            send_ref[to, IN_CV:IN_ROWS, :] = ctx_v


def main_kernel(
    parent_ref,
    resp_len_ref,
    ctx_len_ref,
    places_ref,
    recv_ref,
    send_ref,
    q_f32,
    g_f32,
    q_low,
    g_low,
    k_all,
    v_all,
    chances_all,
    slopes_all,
):
    level = lax.axis_index("level")
    response = lax.div(level, SPLIT)
    part = lax.rem(level, SPLIT)
    live = resp_len_ref[response]
    ctx_live = ctx_len_ref[lax.rem(parent_ref[response], CTX_PER)]

    inner = lax.broadcasted_iota(jnp.int32, (QROWS, HEAD_DIM), 0) % PART
    for source in range(LEVELS):
        both = recv_ref[source, IN_Q:IN_OK, :].astype(f32)
        here = slice(source * QROWS, (source + 1) * QROWS)
        q_f32[here, :] = both[:QROWS]
        place = inner + (source * SPAN + part * PART)
        g_f32[here, :] = jnp.where(place < live, both[QROWS:], 0.0)
        k_all[source * SYS_ROWS : (source + 1) * SYS_ROWS, :] = recv_ref[source, IN_SK:IN_SV, :]
        v_all[source * SYS_ROWS : (source + 1) * SYS_ROWS, :] = recv_ref[source, IN_SV:IN_CK, :]
        start = SYS + source * CTX_ROWS
        k_all[start : start + CTX_ROWS, :] = recv_ref[source, IN_CK:IN_CV, :]
        v_all[start : start + CTX_ROWS, :] = recv_ref[source, IN_CV:IN_ROWS, :]
        start = SYS + CTX + source * SPAN
        k_all[start : start + SPAN, :] = recv_ref[source, IN_OK:IN_OV, :]
        v_all[start : start + SPAN, :] = recv_ref[source, IN_OV:IN_SK, :]
    q_low[...] = q_f32[...].astype(bf16)
    g_low[...] = g_f32[...].astype(bf16)

    rate = SCALING * math.log2(math.e)

    def step(index, unused):
        at = pl.multiple_of(index * BLOCK, BLOCK)
        q_block = q_low[pl.ds(at, BLOCK), :]
        g_block = g_low[pl.ds(at, BLOCK), :]
        places = places_ref[:, pl.ds(at, BLOCK)] + part * PART
        scores = dot(k_all[...], q_block, 1, 1)
        products = dot(v_all[...], g_block, 1, 1)
        ctx_place = lax.broadcasted_iota(jnp.int32, (CTX, BLOCK), 0)
        own_place = lax.broadcasted_iota(jnp.int32, (CH, BLOCK), 0)
        scores = jnp.concatenate(
            [
                scores[:SYS],
                jnp.where(ctx_place < ctx_live, scores[SYS : SYS + CTX], NEGATIVE),
                jnp.where(own_place <= places, scores[SYS + CTX :], NEGATIVE),
            ],
            axis=0,
        )
        top = jnp.max(scores, axis=0, keepdims=True)
        weights = jnp.exp2((scores - top) * rate)
        share = 1.0 / jnp.sum(weights, axis=0, keepdims=True)
        delta = jnp.sum(weights * products, axis=0, keepdims=True) * share
        chances = weights * share
        chances_all[:, pl.ds(at, BLOCK)] = chances.astype(bf16)
        slopes_all[:, pl.ds(at, BLOCK)] = (chances * (products - delta)).astype(bf16)
        return unused

    lax.fori_loop(0, ROWS // BLOCK, step, 0)

    d_key = (dot(slopes_all[...], q_low[...], 1, 0) * SCALING).astype(bf16)
    d_value = dot(chances_all[...], g_low[...], 1, 0).astype(bf16)
    d_query = (dot(k_all[...], slopes_all[...], 0, 0) * SCALING).T
    for to in range(LEVELS):
        for rows, at, low in ((d_key, OUT_SK, 0), (d_value, OUT_SV, 0), (d_key, OUT_CK, SYS), (d_value, OUT_CV, SYS)):
            start = low + to * SYS_ROWS
            send_ref[to, at : at + SYS_ROWS, :] = rows[start : start + SYS_ROWS]
        start = SYS + CTX + to * SPAN
        send_ref[to, OUT_OK:OUT_OV, :] = d_key[start : start + SPAN]
        send_ref[to, OUT_OV:OUT_Q, :] = d_value[start : start + SPAN]
        send_ref[to, OUT_Q:OUT_ROWS, :] = d_query[to * QROWS : (to + 1) * QROWS].astype(bf16)


def finish_kernel(parent_ref, recv_ref, dq_ref, dck_ref, dcv_ref, dok_ref, dov_ref, dsys_ref):
    swap = swap_matrix(SPAN, RESP_DEV)
    rows = []
    for response in range(RESP_DEV):
        for part in range(SPLIT):
            block = recv_ref[response * SPLIT + part, OUT_Q:OUT_ROWS, :].astype(f32)
            rows.append(
                jnp.concatenate(
                    [block[head * PART : (head + 1) * PART] for head in range(HEADS)], axis=1
                )
            )
    whole = jnp.concatenate(rows, axis=0).astype(bf16)
    dq_ref[...] = dot(swap, whole, 1, 0).reshape(SPAN, RESP_DEV, WIDTH)

    twice = jnp.concatenate([swap] * SPLIT, axis=1)
    for low, out_ref in ((OUT_OK, dok_ref), (OUT_OV, dov_ref)):
        stack = jnp.concatenate(
            [
                recv_ref[response * SPLIT + part, low : low + SPAN, :]
                for part in range(SPLIT)
                for response in range(RESP_DEV)
            ],
            axis=0,
        )
        out_ref[...] = dot(twice, stack, 1, 0).reshape(SPAN, RESP_DEV, HEAD_DIM)

    for low, out_ref in ((OUT_CK, dck_ref), (OUT_CV, dcv_ref)):
        out_ref[...] = jnp.zeros_like(out_ref)
        for response in range(RESP_DEV):
            owner = lax.rem(parent_ref[response], CTX_PER)
            block = out_ref[owner]
            for part in range(SPLIT):
                block += recv_ref[response * SPLIT + part, low : low + CTX_ROWS, :].astype(f32)
            out_ref[owner] = block

    total = recv_ref[0, OUT_SK:OUT_CK, :].astype(f32)
    for source in range(1, LEVELS):
        total += recv_ref[source, OUT_SK:OUT_CK, :].astype(f32)
    dsys_ref[...] = jnp.concatenate([total[:SYS_ROWS], total[SYS_ROWS:]], axis=1)


SMEM = pl.BlockSpec(memory_space=pltpu.SMEM)
VMEM = pl.BlockSpec(memory_space=pltpu.VMEM)


def shards(
    queries, out_grad, resp_key, resp_value, sys_key, sys_value, ctx_key, ctx_value, parent, resp_len, ctx_len
):
    send = pl.pallas_call(
        pack_kernel,
        out_shape=jax.ShapeDtypeStruct((LEVELS, IN_ROWS, HEAD_DIM), bf16),
        in_specs=[SMEM] + [VMEM] * 8,
        out_specs=VMEM,
        compiler_params=pltpu.CompilerParams(vmem_limit_bytes=24 * MIB),
        name="pack",
    )(parent, queries, out_grad, resp_key, resp_value, sys_key, sys_value, ctx_key, ctx_value)
    recv = lax.all_to_all(send, "level", 0, 0, tiled=True)

    column = jnp.arange(ROWS, dtype=jnp.int32)
    places = ((column // QROWS) * SPAN + column % PART)[None, :]
    send = pl.pallas_call(
        main_kernel,
        out_shape=jax.ShapeDtypeStruct((LEVELS, OUT_ROWS, HEAD_DIM), bf16),
        in_specs=[SMEM] * 3 + [VMEM] * 2,
        out_specs=VMEM,
        scratch_shapes=[
            pltpu.VMEM((ROWS, HEAD_DIM), f32),
            pltpu.VMEM((ROWS, HEAD_DIM), f32),
            pltpu.VMEM((ROWS, HEAD_DIM), bf16),
            pltpu.VMEM((ROWS, HEAD_DIM), bf16),
            pltpu.VMEM((KEYS, HEAD_DIM), bf16),
            pltpu.VMEM((KEYS, HEAD_DIM), bf16),
            pltpu.VMEM((KEYS, ROWS), bf16),
            pltpu.VMEM((KEYS, ROWS), bf16),
        ],
        compiler_params=pltpu.CompilerParams(vmem_limit_bytes=48 * MIB),
        name="attention",
    )(parent, resp_len, ctx_len, places, recv)
    recv = lax.all_to_all(send, "level", 0, 0, tiled=True)

    d_queries, d_ctx_key, d_ctx_value, d_resp_key, d_resp_value, d_sys = pl.pallas_call(
        finish_kernel,
        out_shape=[
            jax.ShapeDtypeStruct((SPAN, RESP_DEV, WIDTH), f32),
            jax.ShapeDtypeStruct((CTX_PER, CTX_ROWS, HEAD_DIM), f32),
            jax.ShapeDtypeStruct((CTX_PER, CTX_ROWS, HEAD_DIM), f32),
            jax.ShapeDtypeStruct((SPAN, RESP_DEV, HEAD_DIM), f32),
            jax.ShapeDtypeStruct((SPAN, RESP_DEV, HEAD_DIM), f32),
            jax.ShapeDtypeStruct((SYS_ROWS, 2 * HEAD_DIM), f32),
        ],
        in_specs=[SMEM, VMEM],
        out_specs=[VMEM] * 6,
        compiler_params=pltpu.CompilerParams(vmem_limit_bytes=24 * MIB),
        name="finish",
    )(parent, recv)
    d_sys = lax.all_to_all(d_sys[:, None, :], "req", 0, 0, tiled=True)
    d_sys = jnp.sum(d_sys, axis=0)
    return (
        d_queries,
        d_sys[:, :HEAD_DIM],
        d_sys[:, HEAD_DIM:],
        d_ctx_key,
        d_ctx_value,
        d_resp_key,
        d_resp_value,
    )


def solution(mesh):
    return jax.shard_map(
        shards,
        mesh=mesh,
        in_specs=(
            P("level", "req", None),
            P("level", "req", None),
            P("level", "req", None),
            P("level", "req", None),
            P("level", None),
            P("level", None),
            P("req", "level", None),
            P("req", "level", None),
            P("req"),
            P("req"),
            P("req"),
        ),
        out_specs=(
            P("level", "req", None),
            P(("level", "req"), None),
            P(("level", "req"), None),
            P("req", "level", None),
            P("req", "level", None),
            P("level", "req", None),
            P("level", "req", None),
        ),
        check_vma=False,
    )
```

```python
import math

import jax
import jax.numpy as jnp
from jax import lax
from jax.experimental import pallas as pl
from jax.experimental.pallas import tpu as pltpu
from jax.sharding import PartitionSpec as P

HEADS = 7
HEAD_DIM = 128
CTX_PER = 2
LEVELS = 16
RESP_DEV = 8
SPAN = 16
SPLIT = LEVELS // RESP_DEV
PART = SPAN // SPLIT
SYS_ROWS = 32
CTX_ROWS = 32
SYS = SYS_ROWS * LEVELS
CTX = CTX_ROWS * LEVELS
CH = SPAN * LEVELS
KEYS = SYS + CTX + CH
QROWS = PART * HEADS
ROWS = QROWS * LEVELS
WIDTH = HEADS * HEAD_DIM
SCALING = HEAD_DIM**-0.5
NEGATIVE = -1e30
BLOCK = 256
CHUNK = 64
RATE = SCALING * math.log2(math.e)
MIB = 1 << 20

IN_Q = 0
IN_G = IN_Q + QROWS
IN_OK = IN_G + QROWS
IN_OV = IN_OK + SPAN
IN_SK = IN_OV + SPAN
IN_SV = IN_SK + SYS_ROWS
IN_CK = IN_SV + SYS_ROWS
IN_CV = IN_CK + CTX_ROWS
IN_ROWS = IN_CV + CTX_ROWS

OUT_Q = 0
OUT_S = OUT_Q + QROWS
OUT_CK = OUT_S + 8
OUT_CV = OUT_CK + CTX_ROWS
OUT_OK = OUT_CV + CTX_ROWS
OUT_OV = OUT_OK + SPAN
OUT_ROWS = OUT_OV + SPAN

f32 = jnp.float32
bf16 = jnp.bfloat16


def dot(a, b, contract_a, contract_b):
    return lax.dot_general(
        a, b, (((contract_a,), (contract_b,)), ((), ())), preferred_element_type=f32
    )


def swap_matrix(rows_inner, columns_inner):
    size = rows_inner * columns_inner
    row = lax.broadcasted_iota(jnp.int32, (size, size), 0)
    column = lax.broadcasted_iota(jnp.int32, (size, size), 1)
    wanted = (row % columns_inner) * rows_inner + row // columns_inner
    return (column == wanted).astype(bf16)


def flat(ref):
    whole = ref[...].astype(f32)
    return whole.reshape(SPAN * RESP_DEV, whole.shape[2]).astype(bf16)


def pack_kernel(*refs):
    count = len(PACK_SHAPES)
    given, send_ref, held, sems = refs[:count], refs[count], refs[count + 1 : -1], refs[-1]
    copies = [
        pltpu.make_async_copy(given[i], held[i], sems.at[i]) for i in range(count)
    ]
    for copy in copies:
        copy.start()
    for copy in copies:
        copy.wait()
    q_ref, g_ref, rk_ref, rv_ref, sk_ref, sv_ref, ck_ref, cv_ref, parent_ref = held
    swap = swap_matrix(RESP_DEV, SPAN)
    queries = dot(swap, flat(q_ref), 1, 0)
    grads = dot(swap, flat(g_ref), 1, 0)
    own_k = dot(swap, flat(rk_ref), 1, 0).astype(bf16)
    own_v = dot(swap, flat(rv_ref), 1, 0).astype(bf16)
    sys_k = sk_ref[...]
    sys_v = sv_ref[...]
    for response in range(RESP_DEV):
        owner = lax.rem(parent_ref[response], CTX_PER)
        ctx_k = ck_ref[owner]
        ctx_v = cv_ref[owner]
        for part in range(SPLIT):
            to = response * SPLIT + part
            first = response * SPAN + part * PART
            pieces = [
                rows[first : first + PART, head * HEAD_DIM : (head + 1) * HEAD_DIM]
                for rows in (queries, grads)
                for head in range(HEADS)
            ]
            send_ref[to, IN_Q:IN_OK, :] = jnp.concatenate(pieces, axis=0).astype(bf16)
            span = slice(response * SPAN, (response + 1) * SPAN)
            send_ref[to, IN_OK:IN_OV, :] = own_k[span]
            send_ref[to, IN_OV:IN_SK, :] = own_v[span]
            send_ref[to, IN_SK:IN_SV, :] = sys_k
            send_ref[to, IN_SV:IN_CK, :] = sys_v
            send_ref[to, IN_CK:IN_CV, :] = ctx_k
            send_ref[to, IN_CV:IN_ROWS, :] = ctx_v


def collect(resp_len_ref, recv_ref, q_f32, g_f32, q_low, g_low, k_all, v_all):
    level = lax.axis_index("level")
    response = lax.div(level, SPLIT)
    part = lax.rem(level, SPLIT)
    live = resp_len_ref[response]
    inner = lax.broadcasted_iota(jnp.int32, (QROWS, HEAD_DIM), 0) % PART
    for source in range(LEVELS):
        both = recv_ref[source, IN_Q:IN_OK, :].astype(f32)
        here = slice(source * QROWS, (source + 1) * QROWS)
        q_f32[here, :] = both[:QROWS]
        place = inner + (source * SPAN + part * PART)
        g_f32[here, :] = jnp.where(place < live, both[QROWS:], 0.0)
        k_all[source * SYS_ROWS : (source + 1) * SYS_ROWS, :] = recv_ref[source, IN_SK:IN_SV, :]
        v_all[source * SYS_ROWS : (source + 1) * SYS_ROWS, :] = recv_ref[source, IN_SV:IN_CK, :]
        start = SYS + source * CTX_ROWS
        k_all[start : start + CTX_ROWS, :] = recv_ref[source, IN_CK:IN_CV, :]
        v_all[start : start + CTX_ROWS, :] = recv_ref[source, IN_CV:IN_ROWS, :]
        start = SYS + CTX + source * SPAN
        k_all[start : start + SPAN, :] = recv_ref[source, IN_OK:IN_OV, :]
        v_all[start : start + SPAN, :] = recv_ref[source, IN_OV:IN_SK, :]
    q_low[...] = q_f32[...].astype(bf16)
    g_low[...] = g_f32[...].astype(bf16)
    return response, part


def open_score(scores, first, ctx_live, reach):
    if first < SYS:
        return scores
    if first < SYS + CTX:
        row = lax.broadcasted_iota(jnp.int32, scores.shape, 0)
        return jnp.where(row < ctx_live - (first - SYS), scores, NEGATIVE)
    row = lax.broadcasted_iota(jnp.int32, scores.shape, 0)
    return jnp.where(row + (first - SYS - CTX) <= reach, scores, NEGATIVE)


def eights(rows):
    return rows.reshape(rows.shape[0] // 8, 8, rows.shape[1])


def stats_kernel(
    parent_ref,
    resp_len_ref,
    ctx_len_ref,
    places_ref,
    recv_ref,
    sys_ref,
    logsum_ref,
    delta_ref,
    sys_k,
    sys_v,
    q_f32,
    g_f32,
    q_low,
    g_low,
    k_all,
    v_all,
    scores_all,
    products_all,
    chances_all,
    slopes_all,
):
    response, part = collect(resp_len_ref, recv_ref, q_f32, g_f32, q_low, g_low, k_all, v_all)
    ctx_live = ctx_len_ref[lax.rem(parent_ref[response], CTX_PER)]
    for at in range(0, ROWS, BLOCK):
        width = min(BLOCK, ROWS - at)
        columns = slice(at, at + width)
        scores_all[:, columns] = dot(k_all[...], q_low[columns, :], 1, 1)
        products_all[:, columns] = dot(v_all[...], g_low[columns, :], 1, 1)
        reach = places_ref[:, columns] + part * PART
        top = jnp.full((8, width), NEGATIVE, f32)
        for first in range(0, KEYS, CHUNK):
            rows = slice(first, first + CHUNK)
            scores = open_score(scores_all[rows, columns], first, ctx_live, reach)
            top = jnp.maximum(top, jnp.max(eights(scores), axis=0))
        top = jnp.max(top, axis=0, keepdims=True) * RATE
        total = jnp.zeros((8, width), f32)
        delta = jnp.zeros((8, width), f32)
        for first in range(0, KEYS, CHUNK):
            rows = slice(first, first + CHUNK)
            scores = open_score(scores_all[rows, columns], first, ctx_live, reach)
            weights = jnp.exp2(scores * RATE - top)
            if first < SYS:
                scores_all[rows, columns] = weights
            total += jnp.sum(eights(weights), axis=0)
            delta += jnp.sum(eights(weights * products_all[rows, columns]), axis=0)
        total = jnp.sum(total, axis=0, keepdims=True)
        share = 1.0 / total
        delta = jnp.sum(delta, axis=0, keepdims=True) * share
        logsum_ref[:, columns] = top + jnp.log2(total)
        delta_ref[:, columns] = delta
        for first in range(0, SYS, CHUNK):
            rows = slice(first, first + CHUNK)
            chances = scores_all[rows, columns] * share
            chances_all[rows, columns] = chances.astype(bf16)
            slopes_all[rows, columns] = (chances * (products_all[rows, columns] - delta)).astype(bf16)
    sys_k[...] = dot(slopes_all[...], q_low[...], 1, 0) * SCALING
    sys_v[...] = dot(chances_all[...], g_low[...], 1, 0)
    for to in range(SYS_ROWS):
        rows = [grads[pl.ds(to, LEVELS, stride=SYS_ROWS), :] for grads in (sys_k, sys_v)]
        sys_ref[to] = jnp.concatenate(rows, axis=0).astype(bf16)


def grads_kernel(
    parent_ref,
    resp_len_ref,
    ctx_len_ref,
    places_ref,
    recv_ref,
    logsum_ref,
    delta_ref,
    dk_ref,
    dv_ref,
    dq_ref,
    q_f32,
    g_f32,
    q_low,
    g_low,
    k_all,
    v_all,
    scores_all,
    products_all,
    chances_all,
    slopes_all,
):
    response, part = collect(resp_len_ref, recv_ref, q_f32, g_f32, q_low, g_low, k_all, v_all)
    ctx_live = ctx_len_ref[lax.rem(parent_ref[response], CTX_PER)]
    for at in range(0, ROWS, BLOCK):
        width = min(BLOCK, ROWS - at)
        columns = slice(at, at + width)
        scores_all[:, columns] = dot(k_all[...], q_low[columns, :], 1, 1)
        products_all[:, columns] = dot(v_all[...], g_low[columns, :], 1, 1)
        reach = places_ref[:, columns] + part * PART
        logsum = logsum_ref[:, columns]
        delta = delta_ref[:, columns]
        for first in range(0, KEYS, CHUNK):
            rows = slice(first, first + CHUNK)
            scores = open_score(scores_all[rows, columns], first, ctx_live, reach)
            chances = jnp.exp2(scores * RATE - logsum)
            if first >= SYS:
                chances_all[first - SYS : first - SYS + CHUNK, columns] = chances.astype(bf16)
            slopes_all[rows, columns] = (chances * (products_all[rows, columns] - delta)).astype(bf16)
    dk_ref[...] = (dot(slopes_all[SYS:], q_low[...], 1, 0) * SCALING).astype(bf16)
    dv_ref[...] = dot(chances_all[...], g_low[...], 1, 0).astype(bf16)
    dq_ref[...] = (dot(k_all[...], slopes_all[...], 0, 0) * SCALING).T


def gather_kernel(sys_ref, dk_ref, dv_ref, dq_ref, send_ref):
    total = sys_ref[0].astype(f32)
    for source in range(1, SYS_ROWS):
        total += sys_ref[source].astype(f32)
    high = total.astype(bf16).astype(f32)
    rest = total - high
    row = lax.broadcasted_iota(jnp.int32, (8, HEAD_DIM), 0)
    for to in range(LEVELS):
        sums = jnp.zeros((8, HEAD_DIM), f32)
        for at, piece in enumerate((high[to], rest[to], high[LEVELS + to], rest[LEVELS + to])):
            sums = jnp.where(row == at, piece[None, :], sums)
        rows = dq_ref[to * QROWS : (to + 1) * QROWS, :]
        send_ref[to, OUT_Q:OUT_CK, :] = jnp.concatenate([rows, sums], axis=0).astype(bf16)
        ctx = slice(to * CTX_ROWS, (to + 1) * CTX_ROWS)
        send_ref[to, OUT_CK:OUT_CV, :] = dk_ref[ctx, :]
        send_ref[to, OUT_CV:OUT_OK, :] = dv_ref[ctx, :]
        own = slice(CTX + to * SPAN, CTX + (to + 1) * SPAN)
        send_ref[to, OUT_OK:OUT_OV, :] = dk_ref[own, :]
        send_ref[to, OUT_OV:OUT_ROWS, :] = dv_ref[own, :]


def finish_kernel(parent_ref, recv_ref, dq_ref, dck_ref, dcv_ref, dok_ref, dov_ref, dsk_ref, dsv_ref):
    swap = swap_matrix(SPAN, RESP_DEV)
    rows = []
    sums = jnp.zeros((8, HEAD_DIM), f32)
    for response in range(RESP_DEV):
        for part in range(SPLIT):
            block = recv_ref[response * SPLIT + part, OUT_Q:OUT_CK, :].astype(f32)
            sums = sums + block[QROWS:]
            rows.append(
                jnp.concatenate(
                    [block[head * PART : (head + 1) * PART] for head in range(HEADS)], axis=1
                )
            )
    whole = jnp.concatenate(rows, axis=0).astype(bf16)
    dq_ref[...] = dot(swap, whole, 1, 0).reshape(SPAN, RESP_DEV, WIDTH)

    twice = jnp.concatenate([swap] * SPLIT, axis=1)
    for low, out_ref in ((OUT_OK, dok_ref), (OUT_OV, dov_ref)):
        stack = jnp.concatenate(
            [
                recv_ref[response * SPLIT + part, low : low + SPAN, :]
                for part in range(SPLIT)
                for response in range(RESP_DEV)
            ],
            axis=0,
        )
        out_ref[...] = dot(twice, stack, 1, 0).reshape(SPAN, RESP_DEV, HEAD_DIM)

    for low, out_ref in ((OUT_CK, dck_ref), (OUT_CV, dcv_ref)):
        out_ref[...] = jnp.zeros_like(out_ref)
        for response in range(RESP_DEV):
            owner = lax.rem(parent_ref[response], CTX_PER)
            block = out_ref[owner]
            for part in range(SPLIT):
                block += recv_ref[response * SPLIT + part, low : low + CTX_ROWS, :].astype(f32)
            out_ref[owner] = block

    dsk_ref[...] = sums[0:1] + sums[1:2]
    dsv_ref[...] = sums[2:3] + sums[3:4]


SMEM = pl.BlockSpec(memory_space=pltpu.SMEM)
VMEM = pl.BlockSpec(memory_space=pltpu.VMEM)
HBM = pl.BlockSpec(memory_space=pltpu.HBM)
PACK_SHAPES = (
    [((SPAN, RESP_DEV, WIDTH), bf16)] * 2
    + [((SPAN, RESP_DEV, HEAD_DIM), bf16)] * 2
    + [((SYS_ROWS, HEAD_DIM), bf16)] * 2
    + [((CTX_PER, CTX_ROWS, HEAD_DIM), bf16)] * 2
    + [((RESP_DEV,), jnp.int32)]
)


def shards(
    queries, out_grad, resp_key, resp_value, sys_key, sys_value, ctx_key, ctx_value, parent, resp_len, ctx_len
):
    shape = jax.ShapeDtypeStruct
    send = pl.pallas_call(
        pack_kernel,
        out_shape=shape((LEVELS, IN_ROWS, HEAD_DIM), bf16),
        in_specs=[HBM] * len(PACK_SHAPES),
        out_specs=VMEM,
        scratch_shapes=[pltpu.VMEM(*held) for held in PACK_SHAPES[:-1]]
        + [pltpu.SMEM(*PACK_SHAPES[-1]), pltpu.SemaphoreType.DMA((len(PACK_SHAPES),))],
        compiler_params=pltpu.CompilerParams(vmem_limit_bytes=60 * MIB),
        name="pack",
    )(queries, out_grad, resp_key, resp_value, sys_key, sys_value, ctx_key, ctx_value, parent)
    recv = lax.all_to_all(send, "level", 0, 0, tiled=True)

    column = jnp.arange(ROWS, dtype=jnp.int32)
    places = ((column // QROWS) * SPAN + column % PART)[None, :]
    laid_out = [
        pltpu.VMEM((ROWS, HEAD_DIM), f32),
        pltpu.VMEM((ROWS, HEAD_DIM), f32),
        pltpu.VMEM((ROWS, HEAD_DIM), bf16),
        pltpu.VMEM((ROWS, HEAD_DIM), bf16),
        pltpu.VMEM((KEYS, HEAD_DIM), bf16),
        pltpu.VMEM((KEYS, HEAD_DIM), bf16),
        pltpu.VMEM((KEYS, ROWS), f32),
        pltpu.VMEM((KEYS, ROWS), f32),
    ]
    sys_send, logsum, delta = pl.pallas_call(
        stats_kernel,
        out_shape=[
            shape((SYS_ROWS, 2 * LEVELS, HEAD_DIM), bf16),
            shape((1, ROWS), f32),
            shape((1, ROWS), f32),
        ],
        in_specs=[SMEM] * 3 + [VMEM] * 2,
        out_specs=[VMEM] * 3,
        scratch_shapes=[
            pltpu.VMEM((SYS, HEAD_DIM), f32),
            pltpu.VMEM((SYS, HEAD_DIM), f32),
            *laid_out,
            pltpu.VMEM((SYS, ROWS), bf16),
            pltpu.VMEM((SYS, ROWS), bf16),
        ],
        compiler_params=pltpu.CompilerParams(vmem_limit_bytes=40 * MIB),
        cost_estimate=pl.CostEstimate(
            flops=4 * (KEYS + SYS) * ROWS * HEAD_DIM, bytes_accessed=2 * MIB, transcendentals=KEYS * ROWS
        ),
        name="stats",
    )(parent, resp_len, ctx_len, places, recv)
    sys_recv = lax.all_to_all(sys_send, "req", 0, 0, tiled=True)
    d_key, d_value, d_query = pl.pallas_call(
        grads_kernel,
        out_shape=[
            shape((CTX + CH, HEAD_DIM), bf16),
            shape((CTX + CH, HEAD_DIM), bf16),
            shape((ROWS, HEAD_DIM), f32),
        ],
        in_specs=[SMEM] * 3 + [VMEM] * 4,
        out_specs=[VMEM] * 3,
        scratch_shapes=[
            *laid_out,
            pltpu.VMEM((CTX + CH, ROWS), bf16),
            pltpu.VMEM((KEYS, ROWS), bf16),
        ],
        compiler_params=pltpu.CompilerParams(vmem_limit_bytes=40 * MIB),
        cost_estimate=pl.CostEstimate(
            flops=10 * KEYS * ROWS * HEAD_DIM, bytes_accessed=16 * MIB, transcendentals=KEYS * ROWS
        ),
        name="grads",
    )(parent, resp_len, ctx_len, places, recv, logsum, delta)

    send = pl.pallas_call(
        gather_kernel,
        out_shape=shape((LEVELS, OUT_ROWS, HEAD_DIM), bf16),
        in_specs=[VMEM] * 4,
        out_specs=VMEM,
        compiler_params=pltpu.CompilerParams(vmem_limit_bytes=24 * MIB),
        name="gather",
    )(sys_recv, d_key, d_value, d_query)
    recv = lax.all_to_all(send, "level", 0, 0, tiled=True)

    (
        d_queries,
        d_ctx_key,
        d_ctx_value,
        d_resp_key,
        d_resp_value,
        d_sys_key,
        d_sys_value,
    ) = pl.pallas_call(
        finish_kernel,
        out_shape=[
            shape((SPAN, RESP_DEV, WIDTH), f32),
            shape((CTX_PER, CTX_ROWS, HEAD_DIM), f32),
            shape((CTX_PER, CTX_ROWS, HEAD_DIM), f32),
            shape((SPAN, RESP_DEV, HEAD_DIM), f32),
            shape((SPAN, RESP_DEV, HEAD_DIM), f32),
            shape((1, HEAD_DIM), f32),
            shape((1, HEAD_DIM), f32),
        ],
        in_specs=[SMEM, VMEM],
        out_specs=[VMEM] * 7,
        compiler_params=pltpu.CompilerParams(vmem_limit_bytes=24 * MIB),
        name="finish",
    )(parent, recv)
    return (
        d_queries,
        d_sys_key,
        d_sys_value,
        d_ctx_key,
        d_ctx_value,
        d_resp_key,
        d_resp_value,
    )


def solution(mesh):
    return jax.shard_map(
        shards,
        mesh=mesh,
        in_specs=(
            P("level", "req", None),
            P("level", "req", None),
            P("level", "req", None),
            P("level", "req", None),
            P("level", None),
            P("level", None),
            P("req", "level", None),
            P("req", "level", None),
            P("req"),
            P("req"),
            P("req"),
        ),
        out_specs=(
            P("level", "req", None),
            P(("level", "req"), None),
            P(("level", "req"), None),
            P("req", "level", None),
            P("req", "level", None),
            P("level", "req", None),
            P("level", "req", None),
        ),
        check_vma=False,
    )
```

```python
import functools
import math

import jax
import jax.numpy as jnp
from jax import lax
from jax.experimental import pallas as pl
from jax.experimental.pallas import tpu as pltpu
from jax.sharding import PartitionSpec as P

HEADS = 7
HEAD_DIM = 128
CTX_PER = 2
LEVELS = 16
RESP_DEV = 8
SPAN = 16
SPLIT = LEVELS // RESP_DEV
PART = SPAN // SPLIT
SYS_ROWS = 32
CTX_ROWS = 32
SYS = SYS_ROWS * LEVELS
CTX = CTX_ROWS * LEVELS
CH = SPAN * LEVELS
KEYS = SYS + CTX + CH
QROWS = PART * HEADS
ROWS = QROWS * LEVELS
WIDTH = HEADS * HEAD_DIM
SCALING = HEAD_DIM**-0.5
NEGATIVE = -1e30
BLOCK = 256
CHUNK = 64
RATE = SCALING * math.log2(math.e)
MIB = 1 << 20

IN_Q = 0
IN_G = IN_Q + QROWS
IN_OK = IN_G + QROWS
IN_OV = IN_OK + SPAN
IN_SK = IN_OV + SPAN
IN_SV = IN_SK + SYS_ROWS
IN_CK = IN_SV + SYS_ROWS
IN_CV = IN_CK + CTX_ROWS
IN_ROWS = IN_CV + CTX_ROWS

OUT_Q = 0
OUT_S = OUT_Q + QROWS
OUT_CK = OUT_S + 8
OUT_CV = OUT_CK + CTX_ROWS
OUT_OK = OUT_CV + CTX_ROWS
OUT_OV = OUT_OK + SPAN
OUT_ROWS = OUT_OV + SPAN

f32 = jnp.float32
bf16 = jnp.bfloat16


def dot(a, b, contract_a, contract_b):
    return lax.dot_general(
        a, b, (((contract_a,), (contract_b,)), ((), ())), preferred_element_type=f32
    )


def swap_matrix(rows_inner, columns_inner):
    size = rows_inner * columns_inner
    row = lax.broadcasted_iota(jnp.int32, (size, size), 0)
    column = lax.broadcasted_iota(jnp.int32, (size, size), 1)
    wanted = (row % columns_inner) * rows_inner + row // columns_inner
    return (column == wanted).astype(bf16)


def flat(ref):
    whole = ref[...].astype(f32)
    return whole.reshape(SPAN * RESP_DEV, whole.shape[2]).astype(bf16)


def pack_kernel(*refs):
    count = len(PACK_SHAPES)
    given, out_ref = refs[:count], refs[count]
    held, send_ref, sems, out_sems = refs[count + 1 : -3], refs[-3], refs[-2], refs[-1]
    copies = [
        pltpu.make_async_copy(given[i], held[i], sems.at[i]) for i in range(count)
    ]
    for copy in copies:
        copy.start()
    for copy in copies:
        copy.wait()
    q_ref, g_ref, rk_ref, rv_ref, sk_ref, sv_ref, ck_ref, cv_ref, parent_ref = held
    swap = swap_matrix(RESP_DEV, SPAN)
    queries = dot(swap, flat(q_ref), 1, 0)
    grads = dot(swap, flat(g_ref), 1, 0)
    own_k = dot(swap, flat(rk_ref), 1, 0).astype(bf16)
    own_v = dot(swap, flat(rv_ref), 1, 0).astype(bf16)
    sys_k = sk_ref[...]
    sys_v = sv_ref[...]
    copies = []
    for response in range(RESP_DEV):
        owner = lax.rem(parent_ref[response], CTX_PER)
        ctx_k = ck_ref[owner]
        ctx_v = cv_ref[owner]
        for part in range(SPLIT):
            to = response * SPLIT + part
            first = response * SPAN + part * PART
            pieces = [
                rows[first : first + PART, head * HEAD_DIM : (head + 1) * HEAD_DIM]
                for rows in (queries, grads)
                for head in range(HEADS)
            ]
            send_ref[to, IN_Q:IN_OK, :] = jnp.concatenate(pieces, axis=0).astype(bf16)
            span = slice(response * SPAN, (response + 1) * SPAN)
            send_ref[to, IN_OK:IN_OV, :] = own_k[span]
            send_ref[to, IN_OV:IN_SK, :] = own_v[span]
            send_ref[to, IN_SK:IN_SV, :] = sys_k
            send_ref[to, IN_SV:IN_CK, :] = sys_v
            send_ref[to, IN_CK:IN_CV, :] = ctx_k
            send_ref[to, IN_CV:IN_ROWS, :] = ctx_v
        both = pl.ds(response * SPLIT, SPLIT)
        copies.append(
            pltpu.make_async_copy(send_ref.at[both], out_ref.at[both], out_sems.at[response])
        )
        copies[-1].start()
    for copy in copies:
        copy.wait()


def collect(resp_len_ref, recv_ref, q_f32, g_f32, q_low, g_low, k_all, v_all):
    level = lax.axis_index("level")
    response = lax.div(level, SPLIT)
    part = lax.rem(level, SPLIT)
    live = resp_len_ref[response]
    inner = lax.broadcasted_iota(jnp.int32, (QROWS, HEAD_DIM), 0) % PART
    for source in range(LEVELS):
        both = recv_ref[source, IN_Q:IN_OK, :].astype(f32)
        here = slice(source * QROWS, (source + 1) * QROWS)
        q_f32[here, :] = both[:QROWS]
        place = inner + (source * SPAN + part * PART)
        g_f32[here, :] = jnp.where(place < live, both[QROWS:], 0.0)
        k_all[source * SYS_ROWS : (source + 1) * SYS_ROWS, :] = recv_ref[source, IN_SK:IN_SV, :]
        v_all[source * SYS_ROWS : (source + 1) * SYS_ROWS, :] = recv_ref[source, IN_SV:IN_CK, :]
        start = SYS + source * CTX_ROWS
        k_all[start : start + CTX_ROWS, :] = recv_ref[source, IN_CK:IN_CV, :]
        v_all[start : start + CTX_ROWS, :] = recv_ref[source, IN_CV:IN_ROWS, :]
        start = SYS + CTX + source * SPAN
        k_all[start : start + SPAN, :] = recv_ref[source, IN_OK:IN_OV, :]
        v_all[start : start + SPAN, :] = recv_ref[source, IN_OV:IN_SK, :]
    q_low[...] = q_f32[...].astype(bf16)
    g_low[...] = g_f32[...].astype(bf16)
    return response, part


def open_score(scores, first, ctx_live, reach):
    if first < SYS:
        return scores
    if first < SYS + CTX:
        row = lax.broadcasted_iota(jnp.int32, scores.shape, 0)
        return jnp.where(row < ctx_live - (first - SYS), scores, NEGATIVE)
    row = lax.broadcasted_iota(jnp.int32, scores.shape, 0)
    return jnp.where(row + (first - SYS - CTX) <= reach, scores, NEGATIVE)


def stats_kernel(
    parent_ref,
    resp_len_ref,
    ctx_len_ref,
    places_ref,
    recv_ref,
    sys_ref,
    logsum_ref,
    delta_ref,
    sys_k,
    sys_v,
    q_f32,
    g_f32,
    q_low,
    g_low,
    k_all,
    v_all,
    scores_all,
    products_all,
    chances_all,
    slopes_all,
):
    response, part = collect(resp_len_ref, recv_ref, q_f32, g_f32, q_low, g_low, k_all, v_all)
    ctx_live = ctx_len_ref[lax.rem(parent_ref[response], CTX_PER)]
    for at in range(0, ROWS, BLOCK):
        columns = slice(at, min(at + BLOCK, ROWS))
        width = columns.stop - at
        scores_all[:, columns] = dot(k_all[...], q_low[columns, :], 1, 1)
        products_all[:, columns] = dot(v_all[...], g_low[columns, :], 1, 1)
        row = lax.broadcasted_iota(jnp.int32, (8, width), 0)
        reach = places_ref[:, columns] + part * PART - row
        left = ctx_live - row

        def open_eight(first):
            scores = scores_all[first : first + 8, columns]
            if first < SYS:
                return scores
            if first < SYS + CTX:
                return jnp.where(left > first - SYS, scores, NEGATIVE)
            return jnp.where(reach >= first - SYS - CTX, scores, NEGATIVE)

        top = jnp.full((8, width), NEGATIVE, f32)
        total = jnp.zeros((8, width), f32)
        delta = jnp.zeros((8, width), f32)
        for start in range(0, KEYS, CHUNK):
            eights = [open_eight(first) for first in range(start, start + CHUNK, 8)]
            higher = functools.reduce(jnp.maximum, eights, top)
            shrink = jnp.exp2((top - higher) * RATE)
            top, total, delta = higher, total * shrink, delta * shrink
            for index, scores in enumerate(eights):
                first = start + index * 8
                weights = jnp.exp2((scores - top) * RATE)
                total += weights
                delta += weights * products_all[first : first + 8, columns]
        highest = jnp.max(top, axis=0, keepdims=True)
        shrink = jnp.exp2((top - highest) * RATE)
        total = jnp.sum(total * shrink, axis=0, keepdims=True)
        delta = jnp.sum(delta * shrink, axis=0, keepdims=True) / total
        logsum = highest * RATE + jnp.log2(total)
        logsum_ref[:, columns] = logsum
        delta_ref[:, columns] = delta
        for first in range(0, SYS, 16):
            rows = slice(first, first + 16)
            chances = jnp.exp2(scores_all[rows, columns] * RATE - logsum)
            chances_all[rows, columns] = chances.astype(bf16)
            slopes_all[rows, columns] = (chances * (products_all[rows, columns] - delta)).astype(bf16)
    sys_k[...] = dot(slopes_all[...], q_low[...], 1, 0) * SCALING
    sys_v[...] = dot(chances_all[...], g_low[...], 1, 0)
    for to in range(SYS_ROWS):
        rows = [grads[pl.ds(to, LEVELS, stride=SYS_ROWS), :] for grads in (sys_k, sys_v)]
        sys_ref[to] = jnp.concatenate(rows, axis=0).astype(bf16)


def grads_kernel(
    parent_ref,
    resp_len_ref,
    ctx_len_ref,
    places_ref,
    recv_ref,
    logsum_ref,
    delta_ref,
    dk_ref,
    dv_ref,
    dq_ref,
    q_f32,
    g_f32,
    q_low,
    g_low,
    k_all,
    v_all,
    scores_all,
    products_all,
    chances_all,
    slopes_all,
):
    response, part = collect(resp_len_ref, recv_ref, q_f32, g_f32, q_low, g_low, k_all, v_all)
    ctx_live = ctx_len_ref[lax.rem(parent_ref[response], CTX_PER)]
    for at in range(0, ROWS, BLOCK):
        width = min(BLOCK, ROWS - at)
        columns = slice(at, at + width)
        scores_all[:, columns] = dot(k_all[...], q_low[columns, :], 1, 1)
        products_all[:, columns] = dot(v_all[...], g_low[columns, :], 1, 1)
        reach = places_ref[:, columns] + part * PART
        logsum = logsum_ref[:, columns]
        delta = delta_ref[:, columns]
        for first in range(0, KEYS, CHUNK):
            rows = slice(first, first + CHUNK)
            scores = open_score(scores_all[rows, columns], first, ctx_live, reach)
            chances = jnp.exp2(scores * RATE - logsum)
            if first >= SYS:
                chances_all[first - SYS : first - SYS + CHUNK, columns] = chances.astype(bf16)
            slopes_all[rows, columns] = (chances * (products_all[rows, columns] - delta)).astype(bf16)
    dk_ref[...] = (dot(slopes_all[SYS:], q_low[...], 1, 0) * SCALING).astype(bf16)
    dv_ref[...] = dot(chances_all[...], g_low[...], 1, 0).astype(bf16)
    dq_ref[...] = (dot(k_all[...], slopes_all[...], 0, 0) * SCALING).T


def gather_kernel(sys_ref, dk_ref, dv_ref, dq_ref, send_ref):
    total = sys_ref[0].astype(f32)
    for source in range(1, SYS_ROWS):
        total += sys_ref[source].astype(f32)
    high = total.astype(bf16).astype(f32)
    rest = total - high
    row = lax.broadcasted_iota(jnp.int32, (8, HEAD_DIM), 0)
    for to in range(LEVELS):
        sums = jnp.zeros((8, HEAD_DIM), f32)
        for at, piece in enumerate((high[to], rest[to], high[LEVELS + to], rest[LEVELS + to])):
            sums = jnp.where(row == at, piece[None, :], sums)
        rows = dq_ref[to * QROWS : (to + 1) * QROWS, :]
        send_ref[to, OUT_Q:OUT_CK, :] = jnp.concatenate([rows, sums], axis=0).astype(bf16)
        ctx = slice(to * CTX_ROWS, (to + 1) * CTX_ROWS)
        send_ref[to, OUT_CK:OUT_CV, :] = dk_ref[ctx, :]
        send_ref[to, OUT_CV:OUT_OK, :] = dv_ref[ctx, :]
        own = slice(CTX + to * SPAN, CTX + (to + 1) * SPAN)
        send_ref[to, OUT_OK:OUT_OV, :] = dk_ref[own, :]
        send_ref[to, OUT_OV:OUT_ROWS, :] = dv_ref[own, :]


def finish_kernel(parent_ref, swap_ref, recv_ref, dq_ref, dck_ref, dcv_ref, dok_ref, dov_ref, dsk_ref, dsv_ref):
    swap = swap_ref[...]
    rows = []
    sums = jnp.zeros((8, HEAD_DIM), f32)
    for response in range(RESP_DEV):
        for part in range(SPLIT):
            block = recv_ref[response * SPLIT + part, OUT_Q:OUT_CK, :].astype(f32)
            sums = sums + block[QROWS:]
            rows.append(
                jnp.concatenate(
                    [block[head * PART : (head + 1) * PART] for head in range(HEADS)], axis=1
                )
            )
    whole = jnp.concatenate(rows, axis=0).astype(bf16)
    dq_ref[...] = dot(swap, whole, 1, 0).reshape(SPAN, RESP_DEV, WIDTH)

    twice = jnp.concatenate([swap] * SPLIT, axis=1)
    for low, out_ref in ((OUT_OK, dok_ref), (OUT_OV, dov_ref)):
        stack = jnp.concatenate(
            [
                recv_ref[response * SPLIT + part, low : low + SPAN, :]
                for part in range(SPLIT)
                for response in range(RESP_DEV)
            ],
            axis=0,
        )
        out_ref[...] = dot(twice, stack, 1, 0).reshape(SPAN, RESP_DEV, HEAD_DIM)

    for low, out_ref in ((OUT_CK, dck_ref), (OUT_CV, dcv_ref)):
        out_ref[...] = jnp.zeros_like(out_ref)
        for response in range(RESP_DEV):
            owner = lax.rem(parent_ref[response], CTX_PER)
            block = out_ref[owner]
            for part in range(SPLIT):
                block += recv_ref[response * SPLIT + part, low : low + CTX_ROWS, :].astype(f32)
            out_ref[owner] = block

    dsk_ref[...] = sums[0:1] + sums[1:2]
    dsv_ref[...] = sums[2:3] + sums[3:4]


SMEM = pl.BlockSpec(memory_space=pltpu.SMEM)
VMEM = pl.BlockSpec(memory_space=pltpu.VMEM)
HBM = pl.BlockSpec(memory_space=pltpu.HBM)
PACK_SHAPES = (
    [((SPAN, RESP_DEV, WIDTH), bf16)] * 2
    + [((SPAN, RESP_DEV, HEAD_DIM), bf16)] * 2
    + [((SYS_ROWS, HEAD_DIM), bf16)] * 2
    + [((CTX_PER, CTX_ROWS, HEAD_DIM), bf16)] * 2
    + [((RESP_DEV,), jnp.int32)]
)


def shards(
    queries, out_grad, resp_key, resp_value, sys_key, sys_value, ctx_key, ctx_value, parent, resp_len, ctx_len
):
    shape = jax.ShapeDtypeStruct
    send = pl.pallas_call(
        pack_kernel,
        out_shape=shape((LEVELS, IN_ROWS, HEAD_DIM), bf16),
        in_specs=[HBM] * len(PACK_SHAPES),
        out_specs=HBM,
        scratch_shapes=[pltpu.VMEM(*held) for held in PACK_SHAPES[:-1]]
        + [
            pltpu.SMEM(*PACK_SHAPES[-1]),
            pltpu.VMEM((LEVELS, IN_ROWS, HEAD_DIM), bf16),
            pltpu.SemaphoreType.DMA((len(PACK_SHAPES),)),
            pltpu.SemaphoreType.DMA((RESP_DEV,)),
        ],
        compiler_params=pltpu.CompilerParams(vmem_limit_bytes=60 * MIB),
        name="pack",
    )(queries, out_grad, resp_key, resp_value, sys_key, sys_value, ctx_key, ctx_value, parent)
    recv = lax.all_to_all(send, "level", 0, 0, tiled=True)

    column = jnp.arange(ROWS, dtype=jnp.int32)
    places = ((column // QROWS) * SPAN + column % PART)[None, :]
    laid_out = [
        pltpu.VMEM((ROWS, HEAD_DIM), f32),
        pltpu.VMEM((ROWS, HEAD_DIM), f32),
        pltpu.VMEM((ROWS, HEAD_DIM), bf16),
        pltpu.VMEM((ROWS, HEAD_DIM), bf16),
        pltpu.VMEM((KEYS, HEAD_DIM), bf16),
        pltpu.VMEM((KEYS, HEAD_DIM), bf16),
        pltpu.VMEM((KEYS, ROWS), f32),
        pltpu.VMEM((KEYS, ROWS), f32),
    ]
    sys_send, logsum, delta = pl.pallas_call(
        stats_kernel,
        out_shape=[
            shape((SYS_ROWS, 2 * LEVELS, HEAD_DIM), bf16),
            shape((1, ROWS), f32),
            shape((1, ROWS), f32),
        ],
        in_specs=[SMEM] * 3 + [VMEM] * 2,
        out_specs=[VMEM] * 3,
        scratch_shapes=[
            pltpu.VMEM((SYS, HEAD_DIM), f32),
            pltpu.VMEM((SYS, HEAD_DIM), f32),
            *laid_out,
            pltpu.VMEM((SYS, ROWS), bf16),
            pltpu.VMEM((SYS, ROWS), bf16),
        ],
        compiler_params=pltpu.CompilerParams(vmem_limit_bytes=40 * MIB),
        cost_estimate=pl.CostEstimate(
            flops=4 * (KEYS + SYS) * ROWS * HEAD_DIM, bytes_accessed=2 * MIB, transcendentals=KEYS * ROWS
        ),
        name="stats",
    )(parent, resp_len, ctx_len, places, recv)
    sys_recv = lax.all_to_all(sys_send, "req", 0, 0, tiled=True)
    d_key, d_value, d_query = pl.pallas_call(
        grads_kernel,
        out_shape=[
            shape((CTX + CH, HEAD_DIM), bf16),
            shape((CTX + CH, HEAD_DIM), bf16),
            shape((ROWS, HEAD_DIM), f32),
        ],
        in_specs=[SMEM] * 3 + [VMEM] * 4,
        out_specs=[VMEM] * 3,
        scratch_shapes=[
            *laid_out,
            pltpu.VMEM((CTX + CH, ROWS), bf16),
            pltpu.VMEM((KEYS, ROWS), bf16),
        ],
        compiler_params=pltpu.CompilerParams(vmem_limit_bytes=40 * MIB),
        cost_estimate=pl.CostEstimate(
            flops=10 * KEYS * ROWS * HEAD_DIM, bytes_accessed=16 * MIB, transcendentals=KEYS * ROWS
        ),
        name="grads",
    )(parent, resp_len, ctx_len, places, recv, logsum, delta)

    send = pl.pallas_call(
        gather_kernel,
        out_shape=shape((LEVELS, OUT_ROWS, HEAD_DIM), bf16),
        in_specs=[VMEM] * 4,
        out_specs=VMEM,
        compiler_params=pltpu.CompilerParams(vmem_limit_bytes=24 * MIB),
        name="gather",
    )(sys_recv, d_key, d_value, d_query)
    recv = lax.all_to_all(send, "level", 0, 0, tiled=True)

    (
        d_queries,
        d_ctx_key,
        d_ctx_value,
        d_resp_key,
        d_resp_value,
        d_sys_key,
        d_sys_value,
    ) = pl.pallas_call(
        finish_kernel,
        out_shape=[
            shape((SPAN, RESP_DEV, WIDTH), f32),
            shape((CTX_PER, CTX_ROWS, HEAD_DIM), f32),
            shape((CTX_PER, CTX_ROWS, HEAD_DIM), f32),
            shape((SPAN, RESP_DEV, HEAD_DIM), f32),
            shape((SPAN, RESP_DEV, HEAD_DIM), f32),
            shape((1, HEAD_DIM), f32),
            shape((1, HEAD_DIM), f32),
        ],
        in_specs=[SMEM] + [VMEM] * 2,
        out_specs=[VMEM] * 7,
        compiler_params=pltpu.CompilerParams(vmem_limit_bytes=24 * MIB),
        name="finish",
    )(parent, swap_matrix(SPAN, RESP_DEV), recv)
    return (
        d_queries,
        d_sys_key,
        d_sys_value,
        d_ctx_key,
        d_ctx_value,
        d_resp_key,
        d_resp_value,
    )


def solution(mesh):
    return jax.shard_map(
        shards,
        mesh=mesh,
        in_specs=(
            P("level", "req", None),
            P("level", "req", None),
            P("level", "req", None),
            P("level", "req", None),
            P("level", None),
            P("level", None),
            P("req", "level", None),
            P("req", "level", None),
            P("req"),
            P("req"),
            P("req"),
        ),
        out_specs=(
            P("level", "req", None),
            P(("level", "req"), None),
            P(("level", "req"), None),
            P("req", "level", None),
            P("req", "level", None),
            P("level", "req", None),
            P("level", "req", None),
        ),
        check_vma=False,
    )
```

```python
import functools
import math

import jax
import jax.numpy as jnp
from jax import lax
from jax.experimental import pallas as pl
from jax.experimental.pallas import tpu as pltpu
from jax.sharding import PartitionSpec as P

HEADS = 7
HEAD_DIM = 128
CTX_PER = 2
LEVELS = 16
RESP_DEV = 8
SPAN = 16
SPLIT = LEVELS // RESP_DEV
PART = SPAN // SPLIT
SYS_ROWS = 32
CTX_ROWS = 32
SYS = SYS_ROWS * LEVELS
CTX = CTX_ROWS * LEVELS
CH = SPAN * LEVELS
KEYS = SYS + CTX + CH
QROWS = PART * HEADS
ROWS = QROWS * LEVELS
WIDTH = HEADS * HEAD_DIM
SCALING = HEAD_DIM**-0.5
NEGATIVE = -1e30
FIRST_IN = 8
FIRST_SYS = 21
FIRST_OUT = 8
BLOCK = 256
CHUNK = 64
RATE = SCALING * math.log2(math.e)
MIB = 1 << 20

IN_Q = 0
IN_G = IN_Q + QROWS
IN_OK = IN_G + QROWS
IN_OV = IN_OK + SPAN
IN_SK = IN_OV + SPAN
IN_SV = IN_SK + SYS_ROWS
IN_CK = IN_SV + SYS_ROWS
IN_CV = IN_CK + CTX_ROWS
IN_ROWS = IN_CV + CTX_ROWS

OUT_Q = 0
OUT_S = OUT_Q + QROWS
OUT_CK = OUT_S + 8
OUT_CV = OUT_CK + CTX_ROWS
OUT_OK = OUT_CV + CTX_ROWS
OUT_OV = OUT_OK + SPAN
OUT_ROWS = OUT_OV + SPAN

f32 = jnp.float32
bf16 = jnp.bfloat16


def order(first, count):
    return [(first + place) % count for place in range(count)]


def slot(level, first):
    return (level - first) % LEVELS


def dot(a, b, contract_a, contract_b):
    return lax.dot_general(
        a, b, (((contract_a,), (contract_b,)), ((), ())), preferred_element_type=f32
    )


def swap_matrix(rows_inner, columns_inner):
    size = rows_inner * columns_inner
    row = lax.broadcasted_iota(jnp.int32, (size, size), 0)
    column = lax.broadcasted_iota(jnp.int32, (size, size), 1)
    wanted = (row % columns_inner) * rows_inner + row // columns_inner
    return (column == wanted).astype(bf16)


def flat(ref):
    whole = ref[...].astype(f32)
    return whole.reshape(SPAN * RESP_DEV, whole.shape[2]).astype(bf16)


def pack_kernel(*refs):
    count = len(PACK_SHAPES)
    given, out_ref = refs[:count], refs[count]
    held, send_ref, sems, out_sems = refs[count + 1 : -3], refs[-3], refs[-2], refs[-1]
    copies = [
        pltpu.make_async_copy(given[i], held[i], sems.at[i]) for i in range(count)
    ]
    for copy in copies:
        copy.start()
    for copy in copies:
        copy.wait()
    q_ref, g_ref, rk_ref, rv_ref, sk_ref, sv_ref, ck_ref, cv_ref, parent_ref = held
    swap = swap_matrix(RESP_DEV, SPAN)
    queries = dot(swap, flat(q_ref), 1, 0)
    grads = dot(swap, flat(g_ref), 1, 0)
    own_k = dot(swap, flat(rk_ref), 1, 0).astype(bf16)
    own_v = dot(swap, flat(rv_ref), 1, 0).astype(bf16)
    sys_k = sk_ref[...]
    sys_v = sv_ref[...]
    copies = []
    for response in range(RESP_DEV):
        owner = lax.rem(parent_ref[response], CTX_PER)
        ctx_k = ck_ref[owner]
        ctx_v = cv_ref[owner]
        for part in range(SPLIT):
            to = response * SPLIT + part
            first = response * SPAN + part * PART
            pieces = [
                rows[first : first + PART, head * HEAD_DIM : (head + 1) * HEAD_DIM]
                for rows in (queries, grads)
                for head in range(HEADS)
            ]
            send_ref[slot(to, FIRST_IN), IN_Q:IN_OK, :] = jnp.concatenate(pieces, axis=0).astype(bf16)
            span = slice(response * SPAN, (response + 1) * SPAN)
            send_ref[slot(to, FIRST_IN), IN_OK:IN_OV, :] = own_k[span]
            send_ref[slot(to, FIRST_IN), IN_OV:IN_SK, :] = own_v[span]
            send_ref[slot(to, FIRST_IN), IN_SK:IN_SV, :] = sys_k
            send_ref[slot(to, FIRST_IN), IN_SV:IN_CK, :] = sys_v
            send_ref[slot(to, FIRST_IN), IN_CK:IN_CV, :] = ctx_k
            send_ref[slot(to, FIRST_IN), IN_CV:IN_ROWS, :] = ctx_v
        both = pl.ds(slot(response * SPLIT, FIRST_IN), SPLIT)
        copies.append(
            pltpu.make_async_copy(send_ref.at[both], out_ref.at[both], out_sems.at[response])
        )
        copies[-1].start()
    for copy in copies:
        copy.wait()


def collect(resp_len_ref, recv_ref, q_f32, g_f32, q_low, g_low, k_all, v_all):
    level = lax.axis_index("level")
    response = lax.div(level, SPLIT)
    part = lax.rem(level, SPLIT)
    live = resp_len_ref[response]
    inner = lax.broadcasted_iota(jnp.int32, (QROWS, HEAD_DIM), 0) % PART
    for source in range(LEVELS):
        both = recv_ref[slot(source, FIRST_IN), IN_Q:IN_OK, :].astype(f32)
        here = slice(source * QROWS, (source + 1) * QROWS)
        q_f32[here, :] = both[:QROWS]
        place = inner + (source * SPAN + part * PART)
        g_f32[here, :] = jnp.where(place < live, both[QROWS:], 0.0)
        k_all[source * SYS_ROWS : (source + 1) * SYS_ROWS, :] = recv_ref[slot(source, FIRST_IN), IN_SK:IN_SV, :]
        v_all[source * SYS_ROWS : (source + 1) * SYS_ROWS, :] = recv_ref[slot(source, FIRST_IN), IN_SV:IN_CK, :]
        start = SYS + source * CTX_ROWS
        k_all[start : start + CTX_ROWS, :] = recv_ref[slot(source, FIRST_IN), IN_CK:IN_CV, :]
        v_all[start : start + CTX_ROWS, :] = recv_ref[slot(source, FIRST_IN), IN_CV:IN_ROWS, :]
        start = SYS + CTX + source * SPAN
        k_all[start : start + SPAN, :] = recv_ref[slot(source, FIRST_IN), IN_OK:IN_OV, :]
        v_all[start : start + SPAN, :] = recv_ref[slot(source, FIRST_IN), IN_OV:IN_SK, :]
    q_low[...] = q_f32[...].astype(bf16)
    g_low[...] = g_f32[...].astype(bf16)
    return response, part


def open_score(scores, first, ctx_live, reach):
    if first < SYS:
        return scores
    if first < SYS + CTX:
        row = lax.broadcasted_iota(jnp.int32, scores.shape, 0)
        return jnp.where(row < ctx_live - (first - SYS), scores, NEGATIVE)
    row = lax.broadcasted_iota(jnp.int32, scores.shape, 0)
    return jnp.where(row + (first - SYS - CTX) <= reach, scores, NEGATIVE)


def stats_kernel(
    parent_ref,
    resp_len_ref,
    ctx_len_ref,
    places_ref,
    recv_ref,
    sys_ref,
    logsum_ref,
    delta_ref,
    sys_k,
    sys_v,
    q_f32,
    g_f32,
    q_low,
    g_low,
    k_all,
    v_all,
    scores_all,
    products_all,
    chances_all,
    slopes_all,
):
    response, part = collect(resp_len_ref, recv_ref, q_f32, g_f32, q_low, g_low, k_all, v_all)
    ctx_live = ctx_len_ref[lax.rem(parent_ref[response], CTX_PER)]
    for at in range(0, ROWS, BLOCK):
        columns = slice(at, min(at + BLOCK, ROWS))
        width = columns.stop - at
        scores_all[:, columns] = dot(k_all[...], q_low[columns, :], 1, 1)
        products_all[:, columns] = dot(v_all[...], g_low[columns, :], 1, 1)
        row = lax.broadcasted_iota(jnp.int32, (8, width), 0)
        reach = places_ref[:, columns] + part * PART - row
        left = ctx_live - row

        def open_eight(first):
            scores = scores_all[first : first + 8, columns]
            if first < SYS:
                return scores
            if first < SYS + CTX:
                return jnp.where(left > first - SYS, scores, NEGATIVE)
            return jnp.where(reach >= first - SYS - CTX, scores, NEGATIVE)

        top = jnp.full((8, width), NEGATIVE, f32)
        total = jnp.zeros((8, width), f32)
        delta = jnp.zeros((8, width), f32)
        for start in range(0, KEYS, CHUNK):
            eights = [open_eight(first) for first in range(start, start + CHUNK, 8)]
            higher = functools.reduce(jnp.maximum, eights, top)
            shrink = jnp.exp2((top - higher) * RATE)
            top, total, delta = higher, total * shrink, delta * shrink
            for index, scores in enumerate(eights):
                first = start + index * 8
                weights = jnp.exp2((scores - top) * RATE)
                total += weights
                delta += weights * products_all[first : first + 8, columns]
        highest = jnp.max(top, axis=0, keepdims=True)
        shrink = jnp.exp2((top - highest) * RATE)
        total = jnp.sum(total * shrink, axis=0, keepdims=True)
        delta = jnp.sum(delta * shrink, axis=0, keepdims=True) / total
        logsum = highest * RATE + jnp.log2(total)
        logsum_ref[:, columns] = logsum
        delta_ref[:, columns] = delta
        for first in range(0, SYS, 16):
            rows = slice(first, first + 16)
            chances = jnp.exp2(scores_all[rows, columns] * RATE - logsum)
            chances_all[rows, columns] = chances.astype(bf16)
            slopes_all[rows, columns] = (chances * (products_all[rows, columns] - delta)).astype(bf16)
    sys_k[...] = dot(slopes_all[...], q_low[...], 1, 0) * SCALING
    sys_v[...] = dot(chances_all[...], g_low[...], 1, 0)
    for to in range(SYS_ROWS):
        rows = [grads[pl.ds(to, LEVELS, stride=SYS_ROWS), :] for grads in (sys_k, sys_v)]
        sys_ref[(to - FIRST_SYS) % SYS_ROWS] = jnp.concatenate(rows, axis=0).astype(bf16)


def grads_kernel(
    parent_ref,
    resp_len_ref,
    ctx_len_ref,
    places_ref,
    recv_ref,
    logsum_ref,
    delta_ref,
    dk_ref,
    dv_ref,
    dq_ref,
    q_f32,
    g_f32,
    q_low,
    g_low,
    k_all,
    v_all,
    scores_all,
    products_all,
    chances_all,
    slopes_all,
):
    response, part = collect(resp_len_ref, recv_ref, q_f32, g_f32, q_low, g_low, k_all, v_all)
    ctx_live = ctx_len_ref[lax.rem(parent_ref[response], CTX_PER)]
    for at in range(0, ROWS, BLOCK):
        width = min(BLOCK, ROWS - at)
        columns = slice(at, at + width)
        scores_all[:, columns] = dot(k_all[...], q_low[columns, :], 1, 1)
        products_all[:, columns] = dot(v_all[...], g_low[columns, :], 1, 1)
        reach = places_ref[:, columns] + part * PART
        logsum = logsum_ref[:, columns]
        delta = delta_ref[:, columns]
        for first in range(0, KEYS, CHUNK):
            rows = slice(first, first + CHUNK)
            scores = open_score(scores_all[rows, columns], first, ctx_live, reach)
            chances = jnp.exp2(scores * RATE - logsum)
            if first >= SYS:
                chances_all[first - SYS : first - SYS + CHUNK, columns] = chances.astype(bf16)
            slopes_all[rows, columns] = (chances * (products_all[rows, columns] - delta)).astype(bf16)
    dk_ref[...] = (dot(slopes_all[SYS:], q_low[...], 1, 0) * SCALING).astype(bf16)
    dv_ref[...] = dot(chances_all[...], g_low[...], 1, 0).astype(bf16)
    dq_ref[...] = (dot(k_all[...], slopes_all[...], 0, 0) * SCALING).T


def gather_kernel(sys_ref, dk_ref, dv_ref, dq_ref, send_ref):
    total = sys_ref[0].astype(f32)
    for source in range(1, SYS_ROWS):
        total += sys_ref[source].astype(f32)
    high = total.astype(bf16).astype(f32)
    rest = total - high
    row = lax.broadcasted_iota(jnp.int32, (8, HEAD_DIM), 0)
    for to in range(LEVELS):
        sums = jnp.zeros((8, HEAD_DIM), f32)
        for at, piece in enumerate((high[to], rest[to], high[LEVELS + to], rest[LEVELS + to])):
            sums = jnp.where(row == at, piece[None, :], sums)
        rows = dq_ref[to * QROWS : (to + 1) * QROWS, :]
        send_ref[slot(to, FIRST_OUT), OUT_Q:OUT_CK, :] = jnp.concatenate([rows, sums], axis=0).astype(bf16)
        ctx = slice(to * CTX_ROWS, (to + 1) * CTX_ROWS)
        send_ref[slot(to, FIRST_OUT), OUT_CK:OUT_CV, :] = dk_ref[ctx, :]
        send_ref[slot(to, FIRST_OUT), OUT_CV:OUT_OK, :] = dv_ref[ctx, :]
        own = slice(CTX + to * SPAN, CTX + (to + 1) * SPAN)
        send_ref[slot(to, FIRST_OUT), OUT_OK:OUT_OV, :] = dk_ref[own, :]
        send_ref[slot(to, FIRST_OUT), OUT_OV:OUT_ROWS, :] = dv_ref[own, :]


def finish_kernel(parent_ref, swap_ref, recv_ref, dq_ref, dck_ref, dcv_ref, dok_ref, dov_ref, dsk_ref, dsv_ref):
    swap = swap_ref[...]
    rows = []
    sums = jnp.zeros((8, HEAD_DIM), f32)
    for response in range(RESP_DEV):
        for part in range(SPLIT):
            block = recv_ref[slot(response * SPLIT + part, FIRST_OUT), OUT_Q:OUT_CK, :].astype(f32)
            sums = sums + block[QROWS:]
            rows.append(
                jnp.concatenate(
                    [block[head * PART : (head + 1) * PART] for head in range(HEADS)], axis=1
                )
            )
    whole = jnp.concatenate(rows, axis=0).astype(bf16)
    dq_ref[...] = dot(swap, whole, 1, 0).reshape(SPAN, RESP_DEV, WIDTH)

    twice = jnp.concatenate([swap] * SPLIT, axis=1)
    for low, out_ref in ((OUT_OK, dok_ref), (OUT_OV, dov_ref)):
        stack = jnp.concatenate(
            [
                recv_ref[slot(response * SPLIT + part, FIRST_OUT), low : low + SPAN, :]
                for part in range(SPLIT)
                for response in range(RESP_DEV)
            ],
            axis=0,
        )
        out_ref[...] = dot(twice, stack, 1, 0).reshape(SPAN, RESP_DEV, HEAD_DIM)

    for low, out_ref in ((OUT_CK, dck_ref), (OUT_CV, dcv_ref)):
        out_ref[...] = jnp.zeros_like(out_ref)
        for response in range(RESP_DEV):
            owner = lax.rem(parent_ref[response], CTX_PER)
            block = out_ref[owner]
            for part in range(SPLIT):
                block += recv_ref[slot(response * SPLIT + part, FIRST_OUT), low : low + CTX_ROWS, :].astype(f32)
            out_ref[owner] = block

    dsk_ref[...] = sums[0:1] + sums[1:2]
    dsv_ref[...] = sums[2:3] + sums[3:4]


SMEM = pl.BlockSpec(memory_space=pltpu.SMEM)
VMEM = pl.BlockSpec(memory_space=pltpu.VMEM)
HBM = pl.BlockSpec(memory_space=pltpu.HBM)
PACK_SHAPES = (
    [((SPAN, RESP_DEV, WIDTH), bf16)] * 2
    + [((SPAN, RESP_DEV, HEAD_DIM), bf16)] * 2
    + [((SYS_ROWS, HEAD_DIM), bf16)] * 2
    + [((CTX_PER, CTX_ROWS, HEAD_DIM), bf16)] * 2
    + [((RESP_DEV,), jnp.int32)]
)


def shards(
    queries, out_grad, resp_key, resp_value, sys_key, sys_value, ctx_key, ctx_value, parent, resp_len, ctx_len
):
    shape = jax.ShapeDtypeStruct
    send = pl.pallas_call(
        pack_kernel,
        out_shape=shape((LEVELS, IN_ROWS, HEAD_DIM), bf16),
        in_specs=[HBM] * len(PACK_SHAPES),
        out_specs=HBM,
        scratch_shapes=[pltpu.VMEM(*held) for held in PACK_SHAPES[:-1]]
        + [
            pltpu.SMEM(*PACK_SHAPES[-1]),
            pltpu.VMEM((LEVELS, IN_ROWS, HEAD_DIM), bf16),
            pltpu.SemaphoreType.DMA((len(PACK_SHAPES),)),
            pltpu.SemaphoreType.DMA((RESP_DEV,)),
        ],
        compiler_params=pltpu.CompilerParams(vmem_limit_bytes=60 * MIB),
        name="pack",
    )(queries, out_grad, resp_key, resp_value, sys_key, sys_value, ctx_key, ctx_value, parent)
    recv = lax.all_to_all(send, "level", 0, 0, axis_index_groups=[order(FIRST_IN, LEVELS)], tiled=True)

    column = jnp.arange(ROWS, dtype=jnp.int32)
    places = ((column // QROWS) * SPAN + column % PART)[None, :]
    laid_out = [
        pltpu.VMEM((ROWS, HEAD_DIM), f32),
        pltpu.VMEM((ROWS, HEAD_DIM), f32),
        pltpu.VMEM((ROWS, HEAD_DIM), bf16),
        pltpu.VMEM((ROWS, HEAD_DIM), bf16),
        pltpu.VMEM((KEYS, HEAD_DIM), bf16),
        pltpu.VMEM((KEYS, HEAD_DIM), bf16),
        pltpu.VMEM((KEYS, ROWS), f32),
        pltpu.VMEM((KEYS, ROWS), f32),
    ]
    sys_send, logsum, delta = pl.pallas_call(
        stats_kernel,
        out_shape=[
            shape((SYS_ROWS, 2 * LEVELS, HEAD_DIM), bf16),
            shape((1, ROWS), f32),
            shape((1, ROWS), f32),
        ],
        in_specs=[SMEM] * 3 + [VMEM] * 2,
        out_specs=[VMEM] * 3,
        scratch_shapes=[
            pltpu.VMEM((SYS, HEAD_DIM), f32),
            pltpu.VMEM((SYS, HEAD_DIM), f32),
            *laid_out,
            pltpu.VMEM((SYS, ROWS), bf16),
            pltpu.VMEM((SYS, ROWS), bf16),
        ],
        compiler_params=pltpu.CompilerParams(vmem_limit_bytes=40 * MIB),
        cost_estimate=pl.CostEstimate(
            flops=4 * (KEYS + SYS) * ROWS * HEAD_DIM, bytes_accessed=2 * MIB, transcendentals=KEYS * ROWS
        ),
        name="stats",
    )(parent, resp_len, ctx_len, places, recv)
    sys_recv = lax.all_to_all(
        sys_send, "req", 0, 0, axis_index_groups=[order(FIRST_SYS, SYS_ROWS)], tiled=True
    )
    d_key, d_value, d_query = pl.pallas_call(
        grads_kernel,
        out_shape=[
            shape((CTX + CH, HEAD_DIM), bf16),
            shape((CTX + CH, HEAD_DIM), bf16),
            shape((ROWS, HEAD_DIM), f32),
        ],
        in_specs=[SMEM] * 3 + [VMEM] * 4,
        out_specs=[VMEM] * 3,
        scratch_shapes=[
            *laid_out,
            pltpu.VMEM((CTX + CH, ROWS), bf16),
            pltpu.VMEM((KEYS, ROWS), bf16),
        ],
        compiler_params=pltpu.CompilerParams(vmem_limit_bytes=40 * MIB),
        cost_estimate=pl.CostEstimate(
            flops=10 * KEYS * ROWS * HEAD_DIM, bytes_accessed=16 * MIB, transcendentals=KEYS * ROWS
        ),
        name="grads",
    )(parent, resp_len, ctx_len, places, recv, logsum, delta)

    send = pl.pallas_call(
        gather_kernel,
        out_shape=shape((LEVELS, OUT_ROWS, HEAD_DIM), bf16),
        in_specs=[VMEM] * 4,
        out_specs=VMEM,
        compiler_params=pltpu.CompilerParams(vmem_limit_bytes=24 * MIB),
        name="gather",
    )(sys_recv, d_key, d_value, d_query)
    recv = lax.all_to_all(
        send, "level", 0, 0, axis_index_groups=[order(FIRST_OUT, LEVELS)], tiled=True
    )

    (
        d_queries,
        d_ctx_key,
        d_ctx_value,
        d_resp_key,
        d_resp_value,
        d_sys_key,
        d_sys_value,
    ) = pl.pallas_call(
        finish_kernel,
        out_shape=[
            shape((SPAN, RESP_DEV, WIDTH), f32),
            shape((CTX_PER, CTX_ROWS, HEAD_DIM), f32),
            shape((CTX_PER, CTX_ROWS, HEAD_DIM), f32),
            shape((SPAN, RESP_DEV, HEAD_DIM), f32),
            shape((SPAN, RESP_DEV, HEAD_DIM), f32),
            shape((1, HEAD_DIM), f32),
            shape((1, HEAD_DIM), f32),
        ],
        in_specs=[SMEM] + [VMEM] * 2,
        out_specs=[VMEM] * 7,
        compiler_params=pltpu.CompilerParams(vmem_limit_bytes=24 * MIB),
        name="finish",
    )(parent, swap_matrix(SPAN, RESP_DEV), recv)
    return (
        d_queries,
        d_sys_key,
        d_sys_value,
        d_ctx_key,
        d_ctx_value,
        d_resp_key,
        d_resp_value,
    )


def solution(mesh):
    return jax.shard_map(
        shards,
        mesh=mesh,
        in_specs=(
            P("level", "req", None),
            P("level", "req", None),
            P("level", "req", None),
            P("level", "req", None),
            P("level", None),
            P("level", None),
            P("req", "level", None),
            P("req", "level", None),
            P("req"),
            P("req"),
            P("req"),
        ),
        out_specs=(
            P("level", "req", None),
            P(("level", "req"), None),
            P(("level", "req"), None),
            P("req", "level", None),
            P("req", "level", None),
            P("level", "req", None),
            P("level", "req", None),
        ),
        check_vma=False,
    )
```

```python
import functools
import math

import jax
import jax.numpy as jnp
from jax import lax
from jax.experimental import pallas as pl
from jax.experimental.pallas import tpu as pltpu
from jax.sharding import PartitionSpec as P

HEADS = 7
HEAD_DIM = 128
CTX_PER = 2
LEVELS = 16
RESP_DEV = 8
SPAN = 16
SPLIT = LEVELS // RESP_DEV
PART = SPAN // SPLIT
SYS_ROWS = 32
CTX_ROWS = 32
SYS = SYS_ROWS * LEVELS
CTX = CTX_ROWS * LEVELS
CH = SPAN * LEVELS
KEYS = SYS + CTX + CH
QROWS = PART * HEADS
ROWS = QROWS * LEVELS
WIDTH = HEADS * HEAD_DIM
SCALING = HEAD_DIM**-0.5
NEGATIVE = -1e30
FIRST_IN = 8
FIRST_SYS = 21
FIRST_OUT = 12
BLOCK = 256
CHUNK = 64
RATE = SCALING * math.log2(math.e)
MIB = 1 << 20

IN_Q = 0
IN_G = IN_Q + QROWS
IN_OK = IN_G + QROWS
IN_OV = IN_OK + SPAN
IN_SK = IN_OV + SPAN
IN_SV = IN_SK + SYS_ROWS
IN_CK = IN_SV + SYS_ROWS
IN_CV = IN_CK + CTX_ROWS
IN_ROWS = IN_CV + CTX_ROWS

OUT_Q = 0
OUT_S = OUT_Q + QROWS
OUT_CK = OUT_S + 8
OUT_CV = OUT_CK + CTX_ROWS
OUT_OK = OUT_CV + CTX_ROWS
OUT_OV = OUT_OK + SPAN
OUT_ROWS = OUT_OV + SPAN

f32 = jnp.float32
bf16 = jnp.bfloat16


def order(first, count):
    return [(first + place) % count for place in range(count)]


def slot(level, first):
    return (level - first) % LEVELS


def dot(a, b, contract_a, contract_b):
    return lax.dot_general(
        a, b, (((contract_a,), (contract_b,)), ((), ())), preferred_element_type=f32
    )


def swap_matrix(rows_inner, columns_inner):
    size = rows_inner * columns_inner
    row = lax.broadcasted_iota(jnp.int32, (size, size), 0)
    column = lax.broadcasted_iota(jnp.int32, (size, size), 1)
    wanted = (row % columns_inner) * rows_inner + row // columns_inner
    return (column == wanted).astype(bf16)


def flat(ref):
    whole = ref[...].astype(f32)
    return whole.reshape(SPAN * RESP_DEV, whole.shape[2]).astype(bf16)


def pack_kernel(*refs):
    count = len(PACK_SHAPES)
    given, out_ref = refs[:count], refs[count]
    held, send_ref, sems, out_sems = refs[count + 1 : -3], refs[-3], refs[-2], refs[-1]
    copies = [
        pltpu.make_async_copy(given[i], held[i], sems.at[i]) for i in range(count)
    ]
    for copy in copies:
        copy.start()
    for copy in copies:
        copy.wait()
    q_ref, g_ref, rk_ref, rv_ref, sk_ref, sv_ref, ck_ref, cv_ref, parent_ref = held
    swap = swap_matrix(RESP_DEV, SPAN)
    queries = dot(swap, flat(q_ref), 1, 0)
    grads = dot(swap, flat(g_ref), 1, 0)
    own_k = dot(swap, flat(rk_ref), 1, 0).astype(bf16)
    own_v = dot(swap, flat(rv_ref), 1, 0).astype(bf16)
    sys_k = sk_ref[...]
    sys_v = sv_ref[...]
    copies = []
    for response in range(RESP_DEV):
        owner = lax.rem(parent_ref[response], CTX_PER)
        ctx_k = ck_ref[owner]
        ctx_v = cv_ref[owner]
        for part in range(SPLIT):
            to = response * SPLIT + part
            first = response * SPAN + part * PART
            pieces = [
                rows[first : first + PART, head * HEAD_DIM : (head + 1) * HEAD_DIM]
                for rows in (queries, grads)
                for head in range(HEADS)
            ]
            send_ref[slot(to, FIRST_IN), IN_Q:IN_OK, :] = jnp.concatenate(pieces, axis=0).astype(bf16)
            span = slice(response * SPAN, (response + 1) * SPAN)
            send_ref[slot(to, FIRST_IN), IN_OK:IN_OV, :] = own_k[span]
            send_ref[slot(to, FIRST_IN), IN_OV:IN_SK, :] = own_v[span]
            send_ref[slot(to, FIRST_IN), IN_SK:IN_SV, :] = sys_k
            send_ref[slot(to, FIRST_IN), IN_SV:IN_CK, :] = sys_v
            send_ref[slot(to, FIRST_IN), IN_CK:IN_CV, :] = ctx_k
            send_ref[slot(to, FIRST_IN), IN_CV:IN_ROWS, :] = ctx_v
        both = pl.ds(slot(response * SPLIT, FIRST_IN), SPLIT)
        copies.append(
            pltpu.make_async_copy(send_ref.at[both], out_ref.at[both], out_sems.at[response])
        )
        copies[-1].start()
    for copy in copies:
        copy.wait()


def collect(resp_len_ref, recv_ref, q_f32, g_f32, q_low, g_low, k_all, v_all):
    level = lax.axis_index("level")
    response = lax.div(level, SPLIT)
    part = lax.rem(level, SPLIT)
    live = resp_len_ref[response]
    inner = lax.broadcasted_iota(jnp.int32, (QROWS, HEAD_DIM), 0) % PART
    for source in range(LEVELS):
        both = recv_ref[slot(source, FIRST_IN), IN_Q:IN_OK, :].astype(f32)
        here = slice(source * QROWS, (source + 1) * QROWS)
        q_f32[here, :] = both[:QROWS]
        place = inner + (source * SPAN + part * PART)
        g_f32[here, :] = jnp.where(place < live, both[QROWS:], 0.0)
        k_all[source * SYS_ROWS : (source + 1) * SYS_ROWS, :] = recv_ref[slot(source, FIRST_IN), IN_SK:IN_SV, :]
        v_all[source * SYS_ROWS : (source + 1) * SYS_ROWS, :] = recv_ref[slot(source, FIRST_IN), IN_SV:IN_CK, :]
        start = SYS + source * CTX_ROWS
        k_all[start : start + CTX_ROWS, :] = recv_ref[slot(source, FIRST_IN), IN_CK:IN_CV, :]
        v_all[start : start + CTX_ROWS, :] = recv_ref[slot(source, FIRST_IN), IN_CV:IN_ROWS, :]
        start = SYS + CTX + source * SPAN
        k_all[start : start + SPAN, :] = recv_ref[slot(source, FIRST_IN), IN_OK:IN_OV, :]
        v_all[start : start + SPAN, :] = recv_ref[slot(source, FIRST_IN), IN_OV:IN_SK, :]
    q_low[...] = q_f32[...].astype(bf16)
    g_low[...] = g_f32[...].astype(bf16)
    return response, part


def open_score(scores, first, ctx_live, reach):
    if first < SYS:
        return scores
    if first < SYS + CTX:
        row = lax.broadcasted_iota(jnp.int32, scores.shape, 0)
        return jnp.where(row < ctx_live - (first - SYS), scores, NEGATIVE)
    row = lax.broadcasted_iota(jnp.int32, scores.shape, 0)
    return jnp.where(row + (first - SYS - CTX) <= reach, scores, NEGATIVE)


def stats_kernel(
    parent_ref,
    resp_len_ref,
    ctx_len_ref,
    places_ref,
    recv_ref,
    sys_ref,
    logsum_ref,
    delta_ref,
    sys_k,
    sys_v,
    q_f32,
    g_f32,
    q_low,
    g_low,
    k_all,
    v_all,
    scores_all,
    products_all,
    chances_all,
    slopes_all,
):
    response, part = collect(resp_len_ref, recv_ref, q_f32, g_f32, q_low, g_low, k_all, v_all)
    ctx_live = ctx_len_ref[lax.rem(parent_ref[response], CTX_PER)]
    for at in range(0, ROWS, BLOCK):
        columns = slice(at, min(at + BLOCK, ROWS))
        width = columns.stop - at
        scores_all[:, columns] = dot(k_all[...], q_low[columns, :], 1, 1)
        products_all[:, columns] = dot(v_all[...], g_low[columns, :], 1, 1)
        row = lax.broadcasted_iota(jnp.int32, (8, width), 0)
        reach = places_ref[:, columns] + part * PART - row
        left = ctx_live - row

        def open_eight(first):
            scores = scores_all[first : first + 8, columns]
            if first < SYS:
                return scores
            if first < SYS + CTX:
                return jnp.where(left > first - SYS, scores, NEGATIVE)
            return jnp.where(reach >= first - SYS - CTX, scores, NEGATIVE)

        top = jnp.full((8, width), NEGATIVE, f32)
        total = jnp.zeros((8, width), f32)
        delta = jnp.zeros((8, width), f32)
        for start in range(0, KEYS, CHUNK):
            eights = [open_eight(first) for first in range(start, start + CHUNK, 8)]
            higher = functools.reduce(jnp.maximum, eights, top)
            shrink = jnp.exp2((top - higher) * RATE)
            top, total, delta = higher, total * shrink, delta * shrink
            for index, scores in enumerate(eights):
                first = start + index * 8
                weights = jnp.exp2((scores - top) * RATE)
                total += weights
                delta += weights * products_all[first : first + 8, columns]
        highest = jnp.max(top, axis=0, keepdims=True)
        shrink = jnp.exp2((top - highest) * RATE)
        total = jnp.sum(total * shrink, axis=0, keepdims=True)
        delta = jnp.sum(delta * shrink, axis=0, keepdims=True) / total
        logsum = highest * RATE + jnp.log2(total)
        logsum_ref[:, columns] = logsum
        delta_ref[:, columns] = delta
        for first in range(0, SYS, 16):
            rows = slice(first, first + 16)
            chances = jnp.exp2(scores_all[rows, columns] * RATE - logsum)
            chances_all[rows, columns] = chances.astype(bf16)
            slopes_all[rows, columns] = (chances * (products_all[rows, columns] - delta)).astype(bf16)
    sys_k[...] = dot(slopes_all[...], q_low[...], 1, 0) * SCALING
    sys_v[...] = dot(chances_all[...], g_low[...], 1, 0)
    for to in range(SYS_ROWS):
        rows = [grads[pl.ds(to, LEVELS, stride=SYS_ROWS), :] for grads in (sys_k, sys_v)]
        sys_ref[(to - FIRST_SYS) % SYS_ROWS] = jnp.concatenate(rows, axis=0).astype(bf16)


def grads_kernel(
    parent_ref,
    resp_len_ref,
    ctx_len_ref,
    places_ref,
    recv_ref,
    logsum_ref,
    delta_ref,
    dk_ref,
    dv_ref,
    dq_ref,
    q_f32,
    g_f32,
    q_low,
    g_low,
    k_all,
    v_all,
    scores_all,
    products_all,
    chances_all,
    slopes_all,
):
    response, part = collect(resp_len_ref, recv_ref, q_f32, g_f32, q_low, g_low, k_all, v_all)
    ctx_live = ctx_len_ref[lax.rem(parent_ref[response], CTX_PER)]
    for at in range(0, ROWS, BLOCK):
        width = min(BLOCK, ROWS - at)
        columns = slice(at, at + width)
        scores_all[:, columns] = dot(k_all[...], q_low[columns, :], 1, 1)
        products_all[:, columns] = dot(v_all[...], g_low[columns, :], 1, 1)
        reach = places_ref[:, columns] + part * PART
        logsum = logsum_ref[:, columns]
        delta = delta_ref[:, columns]
        for first in range(0, KEYS, CHUNK):
            rows = slice(first, first + CHUNK)
            scores = open_score(scores_all[rows, columns], first, ctx_live, reach)
            chances = jnp.exp2(scores * RATE - logsum)
            if first >= SYS:
                chances_all[first - SYS : first - SYS + CHUNK, columns] = chances.astype(bf16)
            slopes_all[rows, columns] = (chances * (products_all[rows, columns] - delta)).astype(bf16)
    dk_ref[...] = (dot(slopes_all[SYS:], q_low[...], 1, 0) * SCALING).astype(bf16)
    dv_ref[...] = dot(chances_all[...], g_low[...], 1, 0).astype(bf16)
    dq_ref[...] = (dot(k_all[...], slopes_all[...], 0, 0) * SCALING).T


def gather_kernel(sys_ref, dk_ref, dv_ref, dq_ref, send_ref):
    total = sys_ref[0].astype(f32)
    for source in range(1, SYS_ROWS):
        total += sys_ref[source].astype(f32)
    high = total.astype(bf16).astype(f32)
    rest = total - high
    row = lax.broadcasted_iota(jnp.int32, (8, HEAD_DIM), 0)
    for to in range(LEVELS):
        sums = jnp.zeros((8, HEAD_DIM), f32)
        for at, piece in enumerate((high[to], rest[to], high[LEVELS + to], rest[LEVELS + to])):
            sums = jnp.where(row == at, piece[None, :], sums)
        rows = dq_ref[to * QROWS : (to + 1) * QROWS, :]
        send_ref[slot(to, FIRST_OUT), OUT_Q:OUT_CK, :] = jnp.concatenate([rows, sums], axis=0).astype(bf16)
        ctx = slice(to * CTX_ROWS, (to + 1) * CTX_ROWS)
        send_ref[slot(to, FIRST_OUT), OUT_CK:OUT_CV, :] = dk_ref[ctx, :]
        send_ref[slot(to, FIRST_OUT), OUT_CV:OUT_OK, :] = dv_ref[ctx, :]
        own = slice(CTX + to * SPAN, CTX + (to + 1) * SPAN)
        send_ref[slot(to, FIRST_OUT), OUT_OK:OUT_OV, :] = dk_ref[own, :]
        send_ref[slot(to, FIRST_OUT), OUT_OV:OUT_ROWS, :] = dv_ref[own, :]


def finish_kernel(parent_ref, swap_ref, recv_ref, dq_ref, dck_ref, dcv_ref, dok_ref, dov_ref, dsk_ref, dsv_ref):
    swap = swap_ref[...]
    rows = []
    sums = jnp.zeros((8, HEAD_DIM), f32)
    for response in range(RESP_DEV):
        for part in range(SPLIT):
            block = recv_ref[slot(response * SPLIT + part, FIRST_OUT), OUT_Q:OUT_CK, :].astype(f32)
            sums = sums + block[QROWS:]
            rows.append(
                jnp.concatenate(
                    [block[head * PART : (head + 1) * PART] for head in range(HEADS)], axis=1
                )
            )
    whole = jnp.concatenate(rows, axis=0).astype(bf16)
    dq_ref[...] = dot(swap, whole, 1, 0).reshape(SPAN, RESP_DEV, WIDTH)

    twice = jnp.concatenate([swap] * SPLIT, axis=1)
    for low, out_ref in ((OUT_OK, dok_ref), (OUT_OV, dov_ref)):
        stack = jnp.concatenate(
            [
                recv_ref[slot(response * SPLIT + part, FIRST_OUT), low : low + SPAN, :]
                for part in range(SPLIT)
                for response in range(RESP_DEV)
            ],
            axis=0,
        )
        out_ref[...] = dot(twice, stack, 1, 0).reshape(SPAN, RESP_DEV, HEAD_DIM)

    for low, out_ref in ((OUT_CK, dck_ref), (OUT_CV, dcv_ref)):
        out_ref[...] = jnp.zeros_like(out_ref)
        for response in range(RESP_DEV):
            owner = lax.rem(parent_ref[response], CTX_PER)
            block = out_ref[owner]
            for part in range(SPLIT):
                block += recv_ref[slot(response * SPLIT + part, FIRST_OUT), low : low + CTX_ROWS, :].astype(f32)
            out_ref[owner] = block

    dsk_ref[...] = sums[0:1] + sums[1:2]
    dsv_ref[...] = sums[2:3] + sums[3:4]


SMEM = pl.BlockSpec(memory_space=pltpu.SMEM)
VMEM = pl.BlockSpec(memory_space=pltpu.VMEM)
HBM = pl.BlockSpec(memory_space=pltpu.HBM)
PACK_SHAPES = (
    [((SPAN, RESP_DEV, WIDTH), bf16)] * 2
    + [((SPAN, RESP_DEV, HEAD_DIM), bf16)] * 2
    + [((SYS_ROWS, HEAD_DIM), bf16)] * 2
    + [((CTX_PER, CTX_ROWS, HEAD_DIM), bf16)] * 2
    + [((RESP_DEV,), jnp.int32)]
)


def shards(
    queries, out_grad, resp_key, resp_value, sys_key, sys_value, ctx_key, ctx_value, parent, resp_len, ctx_len
):
    shape = jax.ShapeDtypeStruct
    send = pl.pallas_call(
        pack_kernel,
        out_shape=shape((LEVELS, IN_ROWS, HEAD_DIM), bf16),
        in_specs=[HBM] * len(PACK_SHAPES),
        out_specs=HBM,
        scratch_shapes=[pltpu.VMEM(*held) for held in PACK_SHAPES[:-1]]
        + [
            pltpu.SMEM(*PACK_SHAPES[-1]),
            pltpu.VMEM((LEVELS, IN_ROWS, HEAD_DIM), bf16),
            pltpu.SemaphoreType.DMA((len(PACK_SHAPES),)),
            pltpu.SemaphoreType.DMA((RESP_DEV,)),
        ],
        compiler_params=pltpu.CompilerParams(vmem_limit_bytes=60 * MIB),
        name="pack",
    )(queries, out_grad, resp_key, resp_value, sys_key, sys_value, ctx_key, ctx_value, parent)
    recv = lax.all_to_all(send, "level", 0, 0, axis_index_groups=[order(FIRST_IN, LEVELS)], tiled=True)

    column = jnp.arange(ROWS, dtype=jnp.int32)
    places = ((column // QROWS) * SPAN + column % PART)[None, :]
    laid_out = [
        pltpu.VMEM((ROWS, HEAD_DIM), f32),
        pltpu.VMEM((ROWS, HEAD_DIM), f32),
        pltpu.VMEM((ROWS, HEAD_DIM), bf16),
        pltpu.VMEM((ROWS, HEAD_DIM), bf16),
        pltpu.VMEM((KEYS, HEAD_DIM), bf16),
        pltpu.VMEM((KEYS, HEAD_DIM), bf16),
        pltpu.VMEM((KEYS, ROWS), f32),
        pltpu.VMEM((KEYS, ROWS), f32),
    ]
    sys_send, logsum, delta = pl.pallas_call(
        stats_kernel,
        out_shape=[
            shape((SYS_ROWS, 2 * LEVELS, HEAD_DIM), bf16),
            shape((1, ROWS), f32),
            shape((1, ROWS), f32),
        ],
        in_specs=[SMEM] * 3 + [VMEM] * 2,
        out_specs=[VMEM] * 3,
        scratch_shapes=[
            pltpu.VMEM((SYS, HEAD_DIM), f32),
            pltpu.VMEM((SYS, HEAD_DIM), f32),
            *laid_out,
            pltpu.VMEM((SYS, ROWS), bf16),
            pltpu.VMEM((SYS, ROWS), bf16),
        ],
        compiler_params=pltpu.CompilerParams(vmem_limit_bytes=40 * MIB),
        cost_estimate=pl.CostEstimate(
            flops=4 * (KEYS + SYS) * ROWS * HEAD_DIM, bytes_accessed=2 * MIB, transcendentals=KEYS * ROWS
        ),
        name="stats",
    )(parent, resp_len, ctx_len, places, recv)
    sys_recv = lax.all_to_all(
        sys_send, "req", 0, 0, axis_index_groups=[order(FIRST_SYS, SYS_ROWS)], tiled=True
    )
    d_key, d_value, d_query = pl.pallas_call(
        grads_kernel,
        out_shape=[
            shape((CTX + CH, HEAD_DIM), bf16),
            shape((CTX + CH, HEAD_DIM), bf16),
            shape((ROWS, HEAD_DIM), f32),
        ],
        in_specs=[SMEM] * 3 + [VMEM] * 4,
        out_specs=[VMEM] * 3,
        scratch_shapes=[
            *laid_out,
            pltpu.VMEM((CTX + CH, ROWS), bf16),
            pltpu.VMEM((KEYS, ROWS), bf16),
        ],
        compiler_params=pltpu.CompilerParams(vmem_limit_bytes=40 * MIB),
        cost_estimate=pl.CostEstimate(
            flops=10 * KEYS * ROWS * HEAD_DIM, bytes_accessed=16 * MIB, transcendentals=KEYS * ROWS
        ),
        name="grads",
    )(parent, resp_len, ctx_len, places, recv, logsum, delta)

    send = pl.pallas_call(
        gather_kernel,
        out_shape=shape((LEVELS, OUT_ROWS, HEAD_DIM), bf16),
        in_specs=[VMEM] * 4,
        out_specs=VMEM,
        compiler_params=pltpu.CompilerParams(vmem_limit_bytes=24 * MIB),
        name="gather",
    )(sys_recv, d_key, d_value, d_query)
    recv = lax.all_to_all(
        send, "level", 0, 0, axis_index_groups=[order(FIRST_OUT, LEVELS)], tiled=True
    )

    (
        d_queries,
        d_ctx_key,
        d_ctx_value,
        d_resp_key,
        d_resp_value,
        d_sys_key,
        d_sys_value,
    ) = pl.pallas_call(
        finish_kernel,
        out_shape=[
            shape((SPAN, RESP_DEV, WIDTH), f32),
            shape((CTX_PER, CTX_ROWS, HEAD_DIM), f32),
            shape((CTX_PER, CTX_ROWS, HEAD_DIM), f32),
            shape((SPAN, RESP_DEV, HEAD_DIM), f32),
            shape((SPAN, RESP_DEV, HEAD_DIM), f32),
            shape((1, HEAD_DIM), f32),
            shape((1, HEAD_DIM), f32),
        ],
        in_specs=[SMEM] + [VMEM] * 2,
        out_specs=[VMEM] * 7,
        compiler_params=pltpu.CompilerParams(vmem_limit_bytes=24 * MIB),
        name="finish",
    )(parent, swap_matrix(SPAN, RESP_DEV), recv)
    return (
        d_queries,
        d_sys_key,
        d_sys_value,
        d_ctx_key,
        d_ctx_value,
        d_resp_key,
        d_resp_value,
    )


def solution(mesh):
    return jax.shard_map(
        shards,
        mesh=mesh,
        in_specs=(
            P("level", "req", None),
            P("level", "req", None),
            P("level", "req", None),
            P("level", "req", None),
            P("level", None),
            P("level", None),
            P("req", "level", None),
            P("req", "level", None),
            P("req"),
            P("req"),
            P("req"),
        ),
        out_specs=(
            P("level", "req", None),
            P(("level", "req"), None),
            P(("level", "req"), None),
            P("req", "level", None),
            P("req", "level", None),
            P("level", "req", None),
            P("level", "req", None),
        ),
        check_vma=False,
    )
```
